32 devices in a mesh: blk: 4 (over z), member: 8 (over y, x, core).
Axes of the slice: x: 2, y: 2, z: 4, core: 2. Of those that a mesh axis runs over, the one named last changes fastest.
Arguments:
- tokens: bfloat16 [8, 8, 4096], P('member', 'blk'), may hold values from -6 to 6
- cotangent: bfloat16 [8, 8, 4096], P('member', 'blk'), may hold values from -6 to 6
- routes: int32 [8, 8, 8], P('member'), may hold values from 0 to 15, all different within a row; in each aligned block of 8 rows (0 to 7, 8 to 15, ..., all dimensions but the last counted through in order) at most 6 rows name the same one
- gate_wts: float32 [8, 8, 8], P('member'), may hold values from 0.2 to 1
- w_gate: bfloat16 [4, 4096, 4096], P('blk', 'member'), may hold values from -0.09375 to 0.09375
- w_up: bfloat16 [4, 4096, 4096], P('blk', 'member'), may hold values from -0.09375 to 0.09375
- w_down: bfloat16 [4, 4096, 4096], P('blk', 'member'), may hold values from -0.1875 to 0.1875
Outputs:
- layer_out: bfloat16 [8, 8, 4096], P('member', 'blk')
- grad_in: bfloat16 [8, 8, 4096], P('member', 'blk')
The draws below stay inside these ranges and needn't reach their ends.
Inputs may be any that keep to these rules, and one draw needn't show every extreme that they name: `routes`: each token names 8 different experts. Within one token column (the 8 tokens of one index of the first dimension) no expert is named by more than 6 tokens, and in every draw some expert is named by exactly 6 tokens of some column.
All inputs are finite; a program needn't handle non-finite values.
Results may differ from the reference program's by a relative error of at most 0.0058.
Values may be sent and summed in bfloat16 or wider, within the bound.
No kernel may reach another device: no remote copies, remote signals or barrier semaphores. Data moves between devices by JAX's collectives and lax.ppermute only.
A program may use at most 64 MiB of HBM per device.

```python
import math
import jax
import jax.numpy as jnp
import numpy as np
from jax import lax

D = 4096
FF = 1024
TOP = 8
EXP_GRP = 4
CAP = 6
COL = 8
EXPERTS = 16
N_BLK = 4
N_MEMBER = 8


def level_of(rng, extent, pieces, least, largest):
    def one(axis_at, blocks):
        draws = jax.random.uniform(jax.random.fold_in(jax.random.fold_in(rng, 6), axis_at), (blocks,), jnp.float32, least / len(pieces), largest / len(pieces))
        return jnp.repeat(jnp.exp(draws), extent[axis_at] // blocks).reshape((-1,) + (1,) * (len(extent) - axis_at - 1))

    gain = one(*pieces[0])
    for cut in pieces[1:]:
        gain = gain * one(*cut)
    return gain


def routed_block(stream_key, own, number, rows, amount, top, reach, skew):
    ranking = jax.random.permutation(stream_key, amount)
    packed, common = load_shares(amount, rows * top, reach, skew, True), load_shares(amount, rows * top, reach, skew, False)
    places = jnp.arange(amount)

    def named(lengths, turn):
        used = int((lengths > 0).sum())
        fixed = max(1, used // 4)
        passed = fixed + (places - fixed + turn * (used - fixed)) % max(1, amount - fixed)
        return jnp.zeros((amount,), jnp.int32).at[ranking[jnp.where(places < fixed, places, passed)]].set(jnp.asarray(lengths, jnp.int32))

    lengths = jnp.where(number % 4 == 0, named(packed, number // 4), named(common, number - number // 4 - 1))
    mixed = jax.random.permutation(jax.random.fold_in(own, 3), amount)
    donor, taker = mixed[0:amount // 2 * 2:2], mixed[1:amount // 2 * 2:2]
    margin = jnp.minimum(lengths[donor] - 1, reach - lengths[taker]) // 2
    margin = jnp.where((donor == ranking[0]) | (taker == ranking[0]) | (lengths[taker] == 0), 0, jnp.maximum(margin, 0))
    passed = jax.random.randint(jax.random.fold_in(own, 4), (amount // 2,), 0, 1 << 20) % (margin + 1)
    lengths = lengths.at[donor].add(-passed).at[taker].add(passed)
    labels = jnp.searchsorted(jnp.cumsum(lengths), jnp.arange(rows * top), side="right").astype(jnp.int32)
    grid = labels.reshape(top, rows).T
    grid = grid[jax.random.permutation(jax.random.fold_in(own, 1), rows)]
    turn = jax.random.randint(jax.random.fold_in(own, 2), (rows, 1), 0, top)
    return jnp.take_along_axis(grid, (jnp.arange(top)[None, :] + turn) % top, axis=1)


def load_shares(number_of, total, limit, slope, full):
    weights = [(1 << 20) // math.isqrt(rank ** slope) + 1 for rank in range(1, number_of + 1)]
    largest = limit if full else min(limit, max(-(-total // number_of), total * weights[0] // sum(weights)))
    least = 1 if total - largest >= number_of - 1 else 0
    counts, spare = [largest] + [least] * (number_of - 1), total - largest - least * (number_of - 1)
    while spare > 0:
        free = [i for i in range(1, number_of) if counts[i] < largest] or [i for i in range(1, number_of) if counts[i] < limit]
        pool, remaining = sum([weights[i] for i in free]), spare
        for i in free:
            extra = min(limit - counts[i], max(1, remaining * weights[i] // pool), spare)
            counts[i] = counts[i] + extra
            spare = spare - extra
    return np.array(counts)


def bell_draw(key, shape, deviation, most, cuts=(), kind=jnp.bfloat16):
    result = deviation * jax.random.normal(key, shape, jnp.float32)
    if cuts:
        result = result * level_of(key, shape, cuts, -0.22, 0.18)
    return jnp.clip(result, -most, most).astype(kind)


def setup_inputs(seed: int = 0) -> dict:
    key_of = jax.random.split(jax.random.key(seed), 8)
    tokens = bell_draw(key_of[0], (N_MEMBER, COL, D), 1.0, 6.0, ((0, 8), (1, 4)))
    cotangent = bell_draw(key_of[1], (N_MEMBER, COL, D), 1.0, 6.0, ((0, 8), (1, 4)))
    routes_keys = jax.random.split(jax.random.fold_in(key_of[2], 1), N_MEMBER * COL // COL)
    routes_turns = jax.random.permutation(jax.random.fold_in(key_of[2], 3), N_MEMBER * COL // COL)
    routes = jax.vmap(lambda own, number: routed_block(jax.random.fold_in(key_of[2], 2), own, number, COL, EXPERTS, TOP, CAP, 2))(routes_keys, routes_turns).reshape((N_MEMBER, COL, TOP))
    gate_wts = jnp.clip(0.2 + 0.8 * jax.random.uniform(key_of[3], (N_MEMBER, COL, TOP), jnp.float32) ** level_of(key_of[3], (N_MEMBER, COL, TOP), ((0, 8),), -0.2, 0.2), 0.2, 1.0)
    w_gate = bell_draw(key_of[4], (N_BLK, EXP_GRP * FF, D), D ** -0.5, 0.09375, ((0, 4), (1, 8)))
    w_up = bell_draw(key_of[5], (N_BLK, EXP_GRP * FF, D), D ** -0.5, 0.09375, ((0, 4), (1, 8)))
    w_down = bell_draw(key_of[6], (N_BLK, EXP_GRP * FF, D), FF ** -0.5, 0.1875, ((0, 4), (1, 8)))
    return dict(tokens=tokens, cotangent=cotangent, routes=routes, gate_wts=gate_wts, w_gate=w_gate, w_up=w_up, w_down=w_down)


def block_sums(pairs, shards, unit_block):
    total = None
    for left, right in pairs:
        lhs = left.astype(jnp.float32).reshape(left.shape[0], shards, unit_block)
        rhs = right.astype(jnp.float32).reshape(shards, unit_block, right.shape[1])
        term = jnp.einsum("rsh,shd->srd", lhs, rhs, precision=lax.Precision.HIGHEST)
        total = term if total is None else total + term
    rounded = lax.optimization_barrier(total.astype(jnp.bfloat16))
    return jnp.sum(rounded.astype(jnp.float32), axis=0)


def reference(tokens, cotangent, routes, gate_wts, w_gate, w_up, w_down):
    members = tokens.shape[0]
    column = tokens.shape[1]
    model_width = tokens.shape[2]
    experts = EXP_GRP * N_BLK
    shards = N_MEMBER // EXP_GRP
    unit_block = FF // shards
    expert_ids = jnp.arange(experts, dtype=jnp.int32)
    matches = (routes[:, :, :, None] == expert_ids[None, None, None, :]).astype(jnp.int32)
    running = jnp.cumsum(matches.reshape(members, column * TOP, experts), axis=1).reshape(matches.shape) - 1
    slot_ids = jnp.sum(matches * running, axis=3).astype(jnp.int32)
    positions = jnp.broadcast_to(jnp.arange(column, dtype=jnp.int32)[None, :, None], routes.shape)
    column_ids = jnp.broadcast_to(jnp.arange(members, dtype=jnp.int32)[:, None, None], routes.shape)
    index_tab = jnp.full((experts, members, CAP), column, dtype=jnp.int32)
    index_tab = index_tab.at[routes, column_ids, slot_ids].set(positions)
    weight_tab = jnp.zeros((experts, members, CAP), dtype=jnp.float32)
    weight_tab = weight_tab.at[routes, column_ids, slot_ids].set(gate_wts)
    zero_row = jnp.zeros((members, 1, model_width), dtype=tokens.dtype)
    padded_x = jnp.concatenate([tokens, zero_row], axis=1)
    padded_g = jnp.concatenate([cotangent, zero_row], axis=1)
    gate_all = w_gate.reshape(experts, FF, model_width)
    up_all = w_up.reshape(experts, FF, model_width)
    down_all = w_down.reshape(experts, FF, model_width)
    member_rows = jnp.arange(members, dtype=jnp.int32)[:, None]

    def one_expert(carry, inputs):
        acc_out, acc_grad = carry
        index_e, weight_e, gate_e, up_e, down_e = inputs
        row_x = padded_x[member_rows, index_e].reshape(members * CAP, model_width)
        row_g = padded_g[member_rows, index_e].reshape(members * CAP, model_width)
        pre_gate = jnp.dot(row_x, gate_e.T, preferred_element_type=jnp.float32)
        pre_up = jnp.dot(row_x, up_e.T, preferred_element_type=jnp.float32)
        logistic = jax.nn.sigmoid(pre_gate)
        activated = pre_gate * logistic
        hidden = (activated * pre_up).astype(jnp.bfloat16)
        out_sum = block_sums([(hidden, down_e)], shards, unit_block)
        d_hidden = jnp.dot(row_g, down_e.T, preferred_element_type=jnp.float32)
        grad_gate = (d_hidden * pre_up * logistic * (1.0 + pre_gate * (1.0 - logistic))).astype(jnp.bfloat16)
        grad_up = (d_hidden * activated).astype(jnp.bfloat16)
        grad_sum = block_sums([(grad_gate, gate_e), (grad_up, up_e)], shards, unit_block)
        scale = weight_e.reshape(members * CAP, 1)
        acc_out = acc_out.at[member_rows, index_e].add((scale * out_sum).reshape(members, CAP, model_width))
        acc_grad = acc_grad.at[member_rows, index_e].add((scale * grad_sum).reshape(members, CAP, model_width))
        return (acc_out, acc_grad), None

    start = jnp.zeros((members, column + 1, model_width), dtype=jnp.float32)
    (acc_out, acc_grad), _ = lax.scan(one_expert, (start, start), (index_tab, weight_tab, gate_all, up_all, down_all))
    layer_out = acc_out[:, :column].astype(jnp.bfloat16)
    grad_in = acc_grad[:, :column].astype(jnp.bfloat16)
    return (layer_out, grad_in)
```

```python
import jax
import jax.numpy as jnp
from jax import lax
from jax.experimental import pallas as pl
from jax.experimental.pallas import tpu as pltpu
from jax.sharding import PartitionSpec as P

EXP_GRP = 4
CAP = 6
DENSE_TOKENS = 64

CONTRACT_LAST = (((1,), (1,)), ((), ()))
CONTRACT_FIRST = (((0,), (0,)), ((), ()))


def swiglu_kernel(own_ref, other_ref, gate_ref, up_ref, down_ref, own_out, other_out, x_ref, g_ref):
    half = own_ref.shape[0]
    width = gate_ref.shape[1]
    x_ref[:half] = own_ref[:, :width]
    x_ref[half:] = other_ref[:, :width]
    g_ref[:half] = own_ref[:, width:]
    g_ref[half:] = other_ref[:, width:]
    rows_x = x_ref[...]
    rows_g = g_ref[...]
    pre_gate = lax.dot_general(rows_x, gate_ref[...], CONTRACT_LAST, preferred_element_type=jnp.float32)
    pre_up = lax.dot_general(rows_x, up_ref[...], CONTRACT_LAST, preferred_element_type=jnp.float32)
    d_hidden = lax.dot_general(rows_g, down_ref[...], CONTRACT_LAST, preferred_element_type=jnp.float32)
    logistic = jax.nn.sigmoid(pre_gate)
    activated = pre_gate * logistic
    hidden = (activated * pre_up).astype(jnp.bfloat16)
    grad_gate = (d_hidden * pre_up * logistic * (1.0 + pre_gate * (1.0 - logistic))).astype(jnp.bfloat16)
    grad_up = (d_hidden * activated).astype(jnp.bfloat16)
    step = 512
    for at in range(0, width, step):
        part = jnp.dot(hidden, down_ref[:, at : at + step], preferred_element_type=jnp.float32)
        part = part.astype(jnp.bfloat16)
        own_out[:, at : at + step] = part[:half]
        other_out[:, at : at + step] = part[half:]
        part = jnp.dot(grad_gate, gate_ref[:, at : at + step], preferred_element_type=jnp.float32)
        part = part + jnp.dot(grad_up, up_ref[:, at : at + step], preferred_element_type=jnp.float32)
        part = part.astype(jnp.bfloat16)
        own_out[:, width + at : width + at + step] = part[:half]
        other_out[:, width + at : width + at + step] = part[half:]


def swiglu(own, other, gate_local, up_local, down_local):
    half, both = own.shape
    held = [pltpu.with_memory_space_constraint(w, pltpu.VMEM) for w in (gate_local, up_local, down_local)]
    vmem = pl.BlockSpec(memory_space=pltpu.VMEM)
    return pl.pallas_call(
        swiglu_kernel,
        out_shape=[jax.ShapeDtypeStruct((half, both), jnp.bfloat16)] * 2,
        in_specs=[vmem] * 5,
        out_specs=[vmem] * 2,
        scratch_shapes=[pltpu.VMEM((2 * half, both // 2), jnp.bfloat16)] * 2,
        compiler_params=pltpu.CompilerParams(vmem_limit_bytes=24 << 20),
        name="swiglu",
    )(own, other, *held)


def dense_body(tokens, cotangent, routes, gate_wts, w_gate, w_up, w_down):
    blks = lax.axis_size("blk")
    members = lax.axis_size("member")
    shards = members // EXP_GRP
    blk = lax.axis_index("blk")
    _, rows, width = tokens.shape
    both = 2 * width

    def along_blk(value, by):
        return lax.ppermute(value, "blk", [(i, (i + by) % blks) for i in range(blks)])

    def swap(value):
        return lax.ppermute(value, "member", [(i, i ^ 1) for i in range(members)])

    def over_experts(value):
        groups = [[e * shards + s for e in range(EXP_GRP)] for s in range(shards)]
        return lax.all_to_all(value, "member", 0, 0, tiled=True, axis_index_groups=groups)

    held = jnp.concatenate([tokens[0], cotangent[0]], axis=1)
    column = jnp.concatenate([held] + [along_blk(held, k) for k in range(1, blks)], axis=0)
    column_rows = blks * rows
    own = over_experts(jnp.broadcast_to(column[None], (EXP_GRP, column_rows, both)))
    own = own.reshape(EXP_GRP * column_rows, both)
    own_part, other_part = swiglu(own, swap(own), w_gate[0], w_up[0], w_down[0])
    summed = own_part.astype(jnp.float32) + swap(other_part).astype(jnp.float32)
    summed = summed.astype(jnp.bfloat16).reshape(EXP_GRP, column_rows, both)
    back = over_experts(summed)

    places = ((blk - jnp.arange(blks)) % blks)[:, None] * rows + jnp.arange(rows)[None, :]
    places = places.reshape(-1)
    experts = blk * EXP_GRP + jnp.arange(EXP_GRP, dtype=jnp.int32)
    at_place = places[None, :, None, None] == jnp.arange(column_rows)[None, None, :, None]
    named = routes[0][None, None] == experts[:, None, None, None]
    weight = jnp.sum(jnp.where(at_place & named, gate_wts[0][None, None], 0.0), axis=(2, 3))

    total = jnp.sum(back.astype(jnp.float32) * weight[:, :, None], axis=0).reshape(blks, rows, both)
    sent = total.astype(jnp.bfloat16)
    result = total[0]
    for k in range(1, blks):
        result = result + along_blk(sent[k], -k).astype(jnp.float32)
    result = result.astype(jnp.bfloat16)
    return result[None, :, :width], result[None, :, width:]


def slot_layout(route_ids, first_expert, capacity):
    local_ids = route_ids - first_expert
    slot_ids = jnp.arange(EXP_GRP, dtype=jnp.int32)
    matches = (local_ids[None, :, :] == slot_ids[:, None, None]).astype(jnp.int32)
    running = jnp.cumsum(matches.reshape(EXP_GRP, -1), axis=1).reshape(matches.shape) - 1
    places = jnp.arange(capacity, dtype=jnp.int32)
    chosen = (matches[:, None, :, :] == 1) & (running[:, None, :, :] == places[None, :, None, None])
    return chosen.astype(jnp.float32)


def expert_forward(row_block, gate_local, up_local, down_local):
    pre_gate = lax.dot_general(
        row_block, gate_local, CONTRACT_LAST, preferred_element_type=jnp.float32
    )
    pre_up = lax.dot_general(row_block, up_local, CONTRACT_LAST, preferred_element_type=jnp.float32)
    hidden = (pre_gate * jax.nn.sigmoid(pre_gate) * pre_up).astype(jnp.bfloat16)
    partial_value = jnp.dot(hidden, down_local, preferred_element_type=jnp.float32).astype(
        jnp.bfloat16
    )
    return (partial_value, pre_gate, pre_up)


def expert_backward(cot_rows, pre_gate, pre_up, gate_local, up_local, down_local):
    d_hidden = lax.dot_general(
        cot_rows, down_local, CONTRACT_LAST, preferred_element_type=jnp.float32
    )
    logistic = jax.nn.sigmoid(pre_gate)
    activated = pre_gate * logistic
    grad_gate = (d_hidden * pre_up * logistic * (1.0 + pre_gate * (1.0 - logistic))).astype(
        jnp.bfloat16
    )
    grad_up = (d_hidden * activated).astype(jnp.bfloat16)
    partial_value = jnp.dot(grad_gate, gate_local, preferred_element_type=jnp.float32)
    partial_value = partial_value + jnp.dot(grad_up, up_local, preferred_element_type=jnp.float32)
    return partial_value.astype(jnp.bfloat16)


def combine_rows(occupied, slot_weight, returned, shards):
    model_width = returned.shape[2]
    per_slot = jnp.sum(
        returned.astype(jnp.float32).reshape(EXP_GRP, shards, -1, model_width), axis=1
    )
    scaled = per_slot.reshape(-1, model_width) * slot_weight
    return lax.dot_general(
        occupied,
        scaled,
        CONTRACT_FIRST,
        precision=lax.Precision.HIGHEST,
        preferred_element_type=jnp.float32,
    )


def slot_body(tokens, cotangent, routes, gate_wts, w_gate, w_up, w_down):
    col_x, col_g = (
        lax.all_gather(tokens[0], "blk", axis=0, tiled=True),
        lax.all_gather(cotangent[0], "blk", axis=0, tiled=True),
    )
    model_width = col_x.shape[1]
    members = lax.axis_size("member")
    shards = members // EXP_GRP
    layout = slot_layout(routes[0], lax.axis_index("blk") * EXP_GRP, CAP)
    occupied = jnp.sum(layout, axis=3).reshape(EXP_GRP * CAP, -1)
    picker = occupied.astype(jnp.bfloat16)
    slot_weight = jnp.sum(layout * gate_wts[0][None, None, :, :], axis=(2, 3)).reshape(
        EXP_GRP * CAP, 1
    )
    send_x = jnp.dot(picker, col_x, preferred_element_type=jnp.float32).astype(jnp.bfloat16)
    send_g = jnp.dot(picker, col_g, preferred_element_type=jnp.float32).astype(jnp.bfloat16)
    send_x = jnp.repeat(send_x.reshape(EXP_GRP, CAP, model_width), shards, axis=0)
    send_g = jnp.repeat(send_g.reshape(EXP_GRP, CAP, model_width), shards, axis=0)
    gate_local = w_gate[0]
    up_local = w_up[0]
    down_local = w_down[0]
    arrived_x = lax.all_to_all(send_x, "member", split_axis=0, concat_axis=0, tiled=True)
    out_part, pre_gate, pre_up = expert_forward(
        arrived_x.reshape(-1, model_width), gate_local, up_local, down_local
    )
    back_out = lax.all_to_all(
        out_part.reshape(members, CAP, model_width),
        "member",
        split_axis=0,
        concat_axis=0,
        tiled=True,
    )
    arrived_g = lax.all_to_all(send_g, "member", split_axis=0, concat_axis=0, tiled=True)
    grad_part = expert_backward(
        arrived_g.reshape(-1, model_width), pre_gate, pre_up, gate_local, up_local, down_local
    )
    back_grad = lax.all_to_all(
        grad_part.reshape(members, CAP, model_width),
        "member",
        split_axis=0,
        concat_axis=0,
        tiled=True,
    )
    summed_out = combine_rows(occupied, slot_weight, back_out, shards)
    summed_grad = combine_rows(occupied, slot_weight, back_grad, shards)
    out_rows, grad_rows = (
        lax.psum_scatter(summed_out, "blk", scatter_dimension=0, tiled=True),
        lax.psum_scatter(summed_grad, "blk", scatter_dimension=0, tiled=True),
    )
    return (out_rows.astype(jnp.bfloat16)[None], grad_rows.astype(jnp.bfloat16)[None])


def solution(mesh):
    placed = (
        P("member", "blk", None),
        P("member", "blk", None),
        P("member", None, None),
        P("member", None, None),
        P("blk", "member", None),
        P("blk", "member", None),
        P("blk", "member", None),
    )

    def body(tokens, *rest):
        members = lax.axis_size("member")
        count = members * lax.axis_size("blk") * tokens.shape[1]
        dense = count <= DENSE_TOKENS and members == 2 * EXP_GRP
        return (dense_body if dense else slot_body)(tokens, *rest)

    return jax.shard_map(
        body,
        mesh=mesh,
        in_specs=placed,
        out_specs=(P("member", "blk", None), P("member", "blk", None)),
        check_vma=False,
    )
```

```python
import jax
import jax.numpy as jnp
from jax import lax
from jax.experimental import pallas as pl
from jax.experimental.pallas import tpu as pltpu
from jax.sharding import PartitionSpec as P

EXP_GRP = 4
CAP = 6
DENSE_TOKENS = 64
CHUNKS = 4
LOAD_VMEM = 16 << 20
SWIGLU_VMEM = 24 << 20

CONTRACT_LAST = (((1,), (1,)), ((), ()))
CONTRACT_FIRST = (((0,), (0,)), ((), ()))


def load_kernel(*refs):
    count = (len(refs) - 1) // 2
    sems = refs[-1]
    parts = sems.shape[1]
    copies = []
    for i, (far, near) in enumerate(zip(refs[:count], refs[count:-1], strict=True)):
        span = far.shape[0] // parts
        for c in range(parts):
            at = pl.ds(c * span, span)
            copies.append(pltpu.make_async_copy(far.at[at], near.at[at], sems.at[i, c]))
    for copy in copies:
        copy.start()
    for copy in copies:
        copy.wait()


def load(*weights):
    total = sum(w.size * w.dtype.itemsize for w in weights)
    return pl.pallas_call(
        load_kernel,
        out_shape=[pltpu.VMEM(w.shape, w.dtype) for w in weights],
        in_specs=[pl.BlockSpec(memory_space=pltpu.HBM)] * len(weights),
        out_specs=[pl.BlockSpec(memory_space=pltpu.VMEM)] * len(weights),
        scratch_shapes=[pltpu.SemaphoreType.DMA((len(weights), CHUNKS))],
        compiler_params=pltpu.CompilerParams(vmem_limit_bytes=LOAD_VMEM),
        cost_estimate=pl.CostEstimate(flops=0, bytes_accessed=total, transcendentals=0),
        name="load",
    )(*[pltpu.with_memory_space_constraint(w, pltpu.HBM) for w in weights])


def swiglu_kernel(*refs):
    count = (len(refs) - 3) // 2
    pieces, (gate_ref, up_ref, down_ref), results = refs[:count], refs[count : count + 3], refs[count + 3 :]
    width = gate_ref.shape[1]
    rows_x = jnp.concatenate([p[:, :width] for p in pieces], axis=0)
    rows_g = jnp.concatenate([p[:, width:] for p in pieces], axis=0)
    pre_gate = lax.dot_general(rows_x, gate_ref[...], CONTRACT_LAST, preferred_element_type=jnp.float32)
    pre_up = lax.dot_general(rows_x, up_ref[...], CONTRACT_LAST, preferred_element_type=jnp.float32)
    d_hidden = lax.dot_general(rows_g, down_ref[...], CONTRACT_LAST, preferred_element_type=jnp.float32)
    logistic = jax.nn.sigmoid(pre_gate)
    activated = pre_gate * logistic
    hidden = (activated * pre_up).astype(jnp.bfloat16)
    grad_gate = (d_hidden * pre_up * logistic * (1.0 + pre_gate * (1.0 - logistic))).astype(jnp.bfloat16)
    grad_up = (d_hidden * activated).astype(jnp.bfloat16)
    step = 512
    for at in range(0, width, step):
        part = jnp.dot(hidden, down_ref[:, at : at + step], preferred_element_type=jnp.float32)
        grad = jnp.dot(grad_gate, gate_ref[:, at : at + step], preferred_element_type=jnp.float32)
        grad = grad + jnp.dot(grad_up, up_ref[:, at : at + step], preferred_element_type=jnp.float32)
        first = 0
        for result in results:
            rows = result.shape[0]
            result[:, at : at + step] = part[first : first + rows].astype(jnp.bfloat16)
            result[:, width + at : width + at + step] = grad[first : first + rows].astype(jnp.bfloat16)
            first += rows


def swiglu(pieces, weights, out_rows):
    both = pieces[0].shape[1]
    vmem = pl.BlockSpec(memory_space=pltpu.VMEM)
    rows = sum(out_rows)
    flops = 12 * rows * weights[0].size
    return pl.pallas_call(
        swiglu_kernel,
        out_shape=[jax.ShapeDtypeStruct((r, both), jnp.bfloat16) for r in out_rows],
        in_specs=[vmem] * (len(pieces) + len(weights)),
        out_specs=[vmem] * len(out_rows),
        compiler_params=pltpu.CompilerParams(vmem_limit_bytes=SWIGLU_VMEM),
        cost_estimate=pl.CostEstimate(flops=flops, bytes_accessed=6 * weights[0].size, transcendentals=0),
        name="swiglu",
    )(*pieces, *weights)


def dense_body(tokens, cotangent, routes, gate_wts, w_gate, w_up, w_down):
    blks = lax.axis_size("blk")
    members = lax.axis_size("member")
    blk = lax.axis_index("blk")
    member = lax.axis_index("member")
    _, rows, width = tokens.shape
    both = 2 * width
    column_rows = blks * rows
    apart = range(2, members, 2)

    def along_blk(value, by):
        return lax.ppermute(value, "blk", [(i, (i + by) % blks) for i in range(blks)])

    def across(value, bits):
        return lax.ppermute(value, "member", [(i, i ^ bits) for i in range(members)])

    weights = load(w_gate[0], w_up[0], w_down[0])
    held = jnp.concatenate([tokens[0], cotangent[0]], axis=1)
    column = jnp.concatenate([held] + [along_blk(held, k) for k in range(1, blks)], axis=0)
    own = [column] + [across(column, bits) for bits in apart]
    other = [across(piece, 1) for piece in own]
    parts = swiglu(own + other, weights, [column_rows] * (2 * len(own)))
    own_part, other_part = parts[: len(own)], parts[len(own) :]
    summed = [
        (mine.astype(jnp.float32) + across(theirs, 1).astype(jnp.float32)).astype(jnp.bfloat16)
        for mine, theirs in zip(own_part, other_part, strict=True)
    ]
    back = [summed[0]] + [across(piece, bits) for piece, bits in zip(summed[1:], apart, strict=True)]

    places = ((blk - jnp.arange(blks)) % blks)[:, None] * rows + jnp.arange(rows)[None, :]
    slots = (member ^ jnp.arange(0, members, 2)) // 2
    experts = blk * EXP_GRP + slots
    at_place = places.reshape(-1)[None, :, None, None] == jnp.arange(column_rows)[None, None, :, None]
    named = routes[0][None, None] == experts[:, None, None, None]
    weight = jnp.sum(jnp.where(at_place & named, gate_wts[0][None, None], 0.0), axis=(2, 3))

    total = sum(piece.astype(jnp.float32) * weight[i][:, None] for i, piece in enumerate(back))
    total = total.reshape(blks, rows, both)
    sent = total.astype(jnp.bfloat16)
    result = total[0]
    for k in range(1, blks):
        result = result + along_blk(sent[k], -k).astype(jnp.float32)
    result = result.astype(jnp.bfloat16)
    return result[None, :, :width], result[None, :, width:]


def slot_layout(route_ids, first_expert, capacity):
    local_ids = route_ids - first_expert
    slot_ids = jnp.arange(EXP_GRP, dtype=jnp.int32)
    matches = (local_ids[None, :, :] == slot_ids[:, None, None]).astype(jnp.int32)
    running = jnp.cumsum(matches.reshape(EXP_GRP, -1), axis=1).reshape(matches.shape) - 1
    places = jnp.arange(capacity, dtype=jnp.int32)
    chosen = (matches[:, None, :, :] == 1) & (running[:, None, :, :] == places[None, :, None, None])
    return chosen.astype(jnp.float32)


def expert_forward(row_block, gate_local, up_local, down_local):
    pre_gate = lax.dot_general(
        row_block, gate_local, CONTRACT_LAST, preferred_element_type=jnp.float32
    )
    pre_up = lax.dot_general(row_block, up_local, CONTRACT_LAST, preferred_element_type=jnp.float32)
    hidden = (pre_gate * jax.nn.sigmoid(pre_gate) * pre_up).astype(jnp.bfloat16)
    partial_value = jnp.dot(hidden, down_local, preferred_element_type=jnp.float32).astype(
        jnp.bfloat16
    )
    return (partial_value, pre_gate, pre_up)


def expert_backward(cot_rows, pre_gate, pre_up, gate_local, up_local, down_local):
    d_hidden = lax.dot_general(
        cot_rows, down_local, CONTRACT_LAST, preferred_element_type=jnp.float32
    )
    logistic = jax.nn.sigmoid(pre_gate)
    activated = pre_gate * logistic
    grad_gate = (d_hidden * pre_up * logistic * (1.0 + pre_gate * (1.0 - logistic))).astype(
        jnp.bfloat16
    )
    grad_up = (d_hidden * activated).astype(jnp.bfloat16)
    partial_value = jnp.dot(grad_gate, gate_local, preferred_element_type=jnp.float32)
    partial_value = partial_value + jnp.dot(grad_up, up_local, preferred_element_type=jnp.float32)
    return partial_value.astype(jnp.bfloat16)


def combine_rows(occupied, slot_weight, returned, shards):
    model_width = returned.shape[2]
    per_slot = jnp.sum(
        returned.astype(jnp.float32).reshape(EXP_GRP, shards, -1, model_width), axis=1
    )
    scaled = per_slot.reshape(-1, model_width) * slot_weight
    return lax.dot_general(
        occupied,
        scaled,
        CONTRACT_FIRST,
        precision=lax.Precision.HIGHEST,
        preferred_element_type=jnp.float32,
    )


def slot_body(tokens, cotangent, routes, gate_wts, w_gate, w_up, w_down):
    col_x, col_g = (
        lax.all_gather(tokens[0], "blk", axis=0, tiled=True),
        lax.all_gather(cotangent[0], "blk", axis=0, tiled=True),
    )
    model_width = col_x.shape[1]
    members = lax.axis_size("member")
    shards = members // EXP_GRP
    layout = slot_layout(routes[0], lax.axis_index("blk") * EXP_GRP, CAP)
    occupied = jnp.sum(layout, axis=3).reshape(EXP_GRP * CAP, -1)
    picker = occupied.astype(jnp.bfloat16)
    slot_weight = jnp.sum(layout * gate_wts[0][None, None, :, :], axis=(2, 3)).reshape(
        EXP_GRP * CAP, 1
    )
    send_x = jnp.dot(picker, col_x, preferred_element_type=jnp.float32).astype(jnp.bfloat16)
    send_g = jnp.dot(picker, col_g, preferred_element_type=jnp.float32).astype(jnp.bfloat16)
    send_x = jnp.repeat(send_x.reshape(EXP_GRP, CAP, model_width), shards, axis=0)
    send_g = jnp.repeat(send_g.reshape(EXP_GRP, CAP, model_width), shards, axis=0)
    gate_local = w_gate[0]
    up_local = w_up[0]
    down_local = w_down[0]
    arrived_x = lax.all_to_all(send_x, "member", split_axis=0, concat_axis=0, tiled=True)
    out_part, pre_gate, pre_up = expert_forward(
        arrived_x.reshape(-1, model_width), gate_local, up_local, down_local
    )
    back_out = lax.all_to_all(
        out_part.reshape(members, CAP, model_width),
        "member",
        split_axis=0,
        concat_axis=0,
        tiled=True,
    )
    arrived_g = lax.all_to_all(send_g, "member", split_axis=0, concat_axis=0, tiled=True)
    grad_part = expert_backward(
        arrived_g.reshape(-1, model_width), pre_gate, pre_up, gate_local, up_local, down_local
    )
    back_grad = lax.all_to_all(
        grad_part.reshape(members, CAP, model_width),
        "member",
        split_axis=0,
        concat_axis=0,
        tiled=True,
    )
    summed_out = combine_rows(occupied, slot_weight, back_out, shards)
    summed_grad = combine_rows(occupied, slot_weight, back_grad, shards)
    out_rows, grad_rows = (
        lax.psum_scatter(summed_out, "blk", scatter_dimension=0, tiled=True),
        lax.psum_scatter(summed_grad, "blk", scatter_dimension=0, tiled=True),
    )
    return (out_rows.astype(jnp.bfloat16)[None], grad_rows.astype(jnp.bfloat16)[None])


def solution(mesh):
    placed = (
        P("member", "blk", None),
        P("member", "blk", None),
        P("member", None, None),
        P("member", None, None),
        P("blk", "member", None),
        P("blk", "member", None),
        P("blk", "member", None),
    )

    def body(tokens, *rest):
        members = lax.axis_size("member")
        count = members * lax.axis_size("blk") * tokens.shape[1]
        dense = count <= DENSE_TOKENS and members == 2 * EXP_GRP
        return (dense_body if dense else slot_body)(tokens, *rest)

    return jax.shard_map(
        body,
        mesh=mesh,
        in_specs=placed,
        out_specs=(P("member", "blk", None), P("member", "blk", None)),
        check_vma=False,
    )
```

```python
import jax
import jax.numpy as jnp
from jax import lax
from jax.experimental import pallas as pl
from jax.experimental.pallas import tpu as pltpu
from jax.sharding import PartitionSpec as P

EXP_GRP = 4
CAP = 6
DENSE_TOKENS = 64
CHUNKS = 4
LOAD_VMEM = 16 << 20
SWIGLU_VMEM = 24 << 20

CONTRACT_LAST = (((1,), (1,)), ((), ()))
CONTRACT_FIRST = (((0,), (0,)), ((), ()))


def load_kernel(*refs):
    count = (len(refs) - 1) // 2
    sems = refs[-1]
    parts = sems.shape[1]
    copies = []
    for i, (far, near) in enumerate(zip(refs[:count], refs[count:-1], strict=True)):
        span = far.shape[0] // parts
        for c in range(parts):
            at = pl.ds(c * span, span)
            copies.append(pltpu.make_async_copy(far.at[at], near.at[at], sems.at[i, c]))
    for copy in copies:
        copy.start()
    for copy in copies:
        copy.wait()


def load(*weights):
    total = sum(w.size * w.dtype.itemsize for w in weights)
    return pl.pallas_call(
        load_kernel,
        out_shape=[pltpu.VMEM(w.shape, w.dtype) for w in weights],
        in_specs=[pl.BlockSpec(memory_space=pltpu.HBM)] * len(weights),
        out_specs=[pl.BlockSpec(memory_space=pltpu.VMEM)] * len(weights),
        scratch_shapes=[pltpu.SemaphoreType.DMA((len(weights), CHUNKS))],
        compiler_params=pltpu.CompilerParams(vmem_limit_bytes=LOAD_VMEM),
        cost_estimate=pl.CostEstimate(flops=0, bytes_accessed=total, transcendentals=0),
        name="load",
    )(*[pltpu.with_memory_space_constraint(w, pltpu.HBM) for w in weights])


def swiglu_kernel(*refs):
    count = (len(refs) - 3) // 2
    pieces, (gate_ref, up_ref, down_ref), results = refs[:count], refs[count : count + 3], refs[count + 3 :]
    width = gate_ref.shape[1]
    rows_x = jnp.concatenate([p[:, :width] for p in pieces], axis=0)
    rows_g = jnp.concatenate([p[:, width:] for p in pieces], axis=0)
    columns_x = rows_x.T
    pre_gate = jnp.dot(gate_ref[...], columns_x, preferred_element_type=jnp.float32).T
    pre_up = jnp.dot(up_ref[...], columns_x, preferred_element_type=jnp.float32).T
    d_hidden = lax.dot_general(rows_g, down_ref[...], CONTRACT_LAST, preferred_element_type=jnp.float32)
    logistic = jax.nn.sigmoid(pre_gate)
    activated = pre_gate * logistic
    hidden = (activated * pre_up).astype(jnp.bfloat16)
    grad_gate = (d_hidden * pre_up * logistic * (1.0 + pre_gate * (1.0 - logistic))).astype(jnp.bfloat16)
    grad_up = (d_hidden * activated).astype(jnp.bfloat16)
    step = 512
    for at in range(0, width, step):
        part = jnp.dot(hidden, down_ref[:, at : at + step], preferred_element_type=jnp.float32)
        grad = jnp.dot(grad_gate, gate_ref[:, at : at + step], preferred_element_type=jnp.float32)
        grad = grad + jnp.dot(grad_up, up_ref[:, at : at + step], preferred_element_type=jnp.float32)
        first = 0
        for result in results:
            rows = result.shape[0]
            result[:, at : at + step] = part[first : first + rows].astype(jnp.bfloat16)
            result[:, width + at : width + at + step] = grad[first : first + rows].astype(jnp.bfloat16)
            first += rows


def swiglu(pieces, weights, out_rows):
    both = pieces[0].shape[1]
    vmem = pl.BlockSpec(memory_space=pltpu.VMEM)
    rows = sum(out_rows)
    flops = 12 * rows * weights[0].size
    return pl.pallas_call(
        swiglu_kernel,
        out_shape=[jax.ShapeDtypeStruct((r, both), jnp.bfloat16) for r in out_rows],
        in_specs=[vmem] * (len(pieces) + len(weights)),
        out_specs=[vmem] * len(out_rows),
        compiler_params=pltpu.CompilerParams(vmem_limit_bytes=SWIGLU_VMEM),
        cost_estimate=pl.CostEstimate(flops=flops, bytes_accessed=6 * weights[0].size, transcendentals=0),
        name="swiglu",
    )(*pieces, *weights)


def dense_body(tokens, cotangent, routes, gate_wts, w_gate, w_up, w_down):
    blks = lax.axis_size("blk")
    members = lax.axis_size("member")
    blk = lax.axis_index("blk")
    member = lax.axis_index("member")
    _, rows, width = tokens.shape
    both = 2 * width
    column_rows = blks * rows
    apart = range(2, members, 2)

    def along_blk(value, by):
        return lax.ppermute(value, "blk", [(i, (i + by) % blks) for i in range(blks)])

    def across(value, bits):
        return lax.ppermute(value, "member", [(i, i ^ bits) for i in range(members)])

    weights = load(w_gate[0], w_up[0], w_down[0])
    held = lax.optimization_barrier(jnp.concatenate([tokens[0], cotangent[0]], axis=1))
    column = jnp.concatenate([held] + [along_blk(held, k) for k in range(1, blks)], axis=0)
    own = [column] + [across(column, bits) for bits in apart]
    other = [across(piece, 1) for piece in own]
    parts = swiglu(own + other, weights, [column_rows] * (2 * len(own)))
    own_part, other_part = parts[: len(own)], parts[len(own) :]
    summed = [
        (mine.astype(jnp.float32) + across(theirs, 1).astype(jnp.float32)).astype(jnp.bfloat16)
        for mine, theirs in zip(own_part, other_part, strict=True)
    ]
    back = [summed[0]] + [across(piece, bits) for piece, bits in zip(summed[1:], apart, strict=True)]

    places = ((blk - jnp.arange(blks)) % blks)[:, None] * rows + jnp.arange(rows)[None, :]
    slots = (member ^ jnp.arange(0, members, 2)) // 2
    experts = blk * EXP_GRP + slots
    at_place = places.reshape(-1)[None, :, None, None] == jnp.arange(column_rows)[None, None, :, None]
    named = routes[0][None, None] == experts[:, None, None, None]
    weight = jnp.sum(jnp.where(at_place & named, gate_wts[0][None, None], 0.0), axis=(2, 3))

    total = sum(piece.astype(jnp.float32) * weight[i][:, None] for i, piece in enumerate(back))
    total = total.reshape(blks, rows, both)
    sent = total.astype(jnp.bfloat16)
    result = total[0]
    for k in range(blks - 1, 0, -1):
        result = result + along_blk(sent[k], -k).astype(jnp.float32)
    result = result.astype(jnp.bfloat16)
    return result[None, :, :width], result[None, :, width:]


def slot_layout(route_ids, first_expert, capacity):
    local_ids = route_ids - first_expert
    slot_ids = jnp.arange(EXP_GRP, dtype=jnp.int32)
    matches = (local_ids[None, :, :] == slot_ids[:, None, None]).astype(jnp.int32)
    running = jnp.cumsum(matches.reshape(EXP_GRP, -1), axis=1).reshape(matches.shape) - 1
    places = jnp.arange(capacity, dtype=jnp.int32)
    chosen = (matches[:, None, :, :] == 1) & (running[:, None, :, :] == places[None, :, None, None])
    return chosen.astype(jnp.float32)


def expert_forward(row_block, gate_local, up_local, down_local):
    pre_gate = lax.dot_general(
        row_block, gate_local, CONTRACT_LAST, preferred_element_type=jnp.float32
    )
    pre_up = lax.dot_general(row_block, up_local, CONTRACT_LAST, preferred_element_type=jnp.float32)
    hidden = (pre_gate * jax.nn.sigmoid(pre_gate) * pre_up).astype(jnp.bfloat16)
    partial_value = jnp.dot(hidden, down_local, preferred_element_type=jnp.float32).astype(
        jnp.bfloat16
    )
    return (partial_value, pre_gate, pre_up)


def expert_backward(cot_rows, pre_gate, pre_up, gate_local, up_local, down_local):
    d_hidden = lax.dot_general(
        cot_rows, down_local, CONTRACT_LAST, preferred_element_type=jnp.float32
    )
    logistic = jax.nn.sigmoid(pre_gate)
    activated = pre_gate * logistic
    grad_gate = (d_hidden * pre_up * logistic * (1.0 + pre_gate * (1.0 - logistic))).astype(
        jnp.bfloat16
    )
    grad_up = (d_hidden * activated).astype(jnp.bfloat16)
    partial_value = jnp.dot(grad_gate, gate_local, preferred_element_type=jnp.float32)
    partial_value = partial_value + jnp.dot(grad_up, up_local, preferred_element_type=jnp.float32)
    return partial_value.astype(jnp.bfloat16)


def combine_rows(occupied, slot_weight, returned, shards):
    model_width = returned.shape[2]
    per_slot = jnp.sum(
        returned.astype(jnp.float32).reshape(EXP_GRP, shards, -1, model_width), axis=1
    )
    scaled = per_slot.reshape(-1, model_width) * slot_weight
    return lax.dot_general(
        occupied,
        scaled,
        CONTRACT_FIRST,
        precision=lax.Precision.HIGHEST,
        preferred_element_type=jnp.float32,
    )


def slot_body(tokens, cotangent, routes, gate_wts, w_gate, w_up, w_down):
    col_x, col_g = (
        lax.all_gather(tokens[0], "blk", axis=0, tiled=True),
        lax.all_gather(cotangent[0], "blk", axis=0, tiled=True),
    )
    model_width = col_x.shape[1]
    members = lax.axis_size("member")
    shards = members // EXP_GRP
    layout = slot_layout(routes[0], lax.axis_index("blk") * EXP_GRP, CAP)
    occupied = jnp.sum(layout, axis=3).reshape(EXP_GRP * CAP, -1)
    picker = occupied.astype(jnp.bfloat16)
    slot_weight = jnp.sum(layout * gate_wts[0][None, None, :, :], axis=(2, 3)).reshape(
        EXP_GRP * CAP, 1
    )
    send_x = jnp.dot(picker, col_x, preferred_element_type=jnp.float32).astype(jnp.bfloat16)
    send_g = jnp.dot(picker, col_g, preferred_element_type=jnp.float32).astype(jnp.bfloat16)
    send_x = jnp.repeat(send_x.reshape(EXP_GRP, CAP, model_width), shards, axis=0)
    send_g = jnp.repeat(send_g.reshape(EXP_GRP, CAP, model_width), shards, axis=0)
    gate_local = w_gate[0]
    up_local = w_up[0]
    down_local = w_down[0]
    arrived_x = lax.all_to_all(send_x, "member", split_axis=0, concat_axis=0, tiled=True)
    out_part, pre_gate, pre_up = expert_forward(
        arrived_x.reshape(-1, model_width), gate_local, up_local, down_local
    )
    back_out = lax.all_to_all(
        out_part.reshape(members, CAP, model_width),
        "member",
        split_axis=0,
        concat_axis=0,
        tiled=True,
    )
    arrived_g = lax.all_to_all(send_g, "member", split_axis=0, concat_axis=0, tiled=True)
    grad_part = expert_backward(
        arrived_g.reshape(-1, model_width), pre_gate, pre_up, gate_local, up_local, down_local
    )
    back_grad = lax.all_to_all(
        grad_part.reshape(members, CAP, model_width),
        "member",
        split_axis=0,
        concat_axis=0,
        tiled=True,
    )
    summed_out = combine_rows(occupied, slot_weight, back_out, shards)
    summed_grad = combine_rows(occupied, slot_weight, back_grad, shards)
    out_rows, grad_rows = (
        lax.psum_scatter(summed_out, "blk", scatter_dimension=0, tiled=True),
        lax.psum_scatter(summed_grad, "blk", scatter_dimension=0, tiled=True),
    )
    return (out_rows.astype(jnp.bfloat16)[None], grad_rows.astype(jnp.bfloat16)[None])


def solution(mesh):
    placed = (
        P("member", "blk", None),
        P("member", "blk", None),
        P("member", None, None),
        P("member", None, None),
        P("blk", "member", None),
        P("blk", "member", None),
        P("blk", "member", None),
    )

    def body(tokens, *rest):
        members = lax.axis_size("member")
        count = members * lax.axis_size("blk") * tokens.shape[1]
        dense = count <= DENSE_TOKENS and members == 2 * EXP_GRP
        return (dense_body if dense else slot_body)(tokens, *rest)

    return jax.shard_map(
        body,
        mesh=mesh,
        in_specs=placed,
        out_specs=(P("member", "blk", None), P("member", "blk", None)),
        check_vma=False,
    )
```

```python
import functools

import jax
import jax.numpy as jnp
from jax import lax
from jax.experimental import pallas as pl
from jax.experimental.pallas import tpu as pltpu
from jax.sharding import PartitionSpec as P

EXP_GRP = 4
CAP = 6
DENSE_TOKENS = 64
CHUNKS = 4
TURN = 512
LOAD_VMEM = 16 << 20
SWIGLU_VMEM = 24 << 20

CONTRACT_LAST = (((1,), (1,)), ((), ()))
CONTRACT_FIRST = (((0,), (0,)), ((), ()))


def load_kernel(*refs):
    count = (len(refs) - 1) // 2
    sems = refs[-1]
    parts = sems.shape[1]
    copies = []
    for i, (far, near) in enumerate(zip(refs[:count], refs[count:-1], strict=True)):
        span = far.shape[0] // parts
        for c in range(parts):
            at = pl.ds(c * span, span)
            copies.append(pltpu.make_async_copy(far.at[at], near.at[at], sems.at[i, c]))
    for copy in copies:
        copy.start()
    for copy in copies:
        copy.wait()


def load(*weights):
    total = sum(w.size * w.dtype.itemsize for w in weights)
    return pl.pallas_call(
        load_kernel,
        out_shape=[pltpu.VMEM(w.shape, w.dtype) for w in weights],
        in_specs=[pl.BlockSpec(memory_space=pltpu.HBM)] * len(weights),
        out_specs=[pl.BlockSpec(memory_space=pltpu.VMEM)] * len(weights),
        scratch_shapes=[pltpu.SemaphoreType.DMA((len(weights), CHUNKS))],
        compiler_params=pltpu.CompilerParams(vmem_limit_bytes=LOAD_VMEM),
        cost_estimate=pl.CostEstimate(flops=0, bytes_accessed=total, transcendentals=0),
        name="load",
    )(*[pltpu.with_memory_space_constraint(w, pltpu.HBM) for w in weights])


def turn_kernel(held, count, _, *refs):
    far, near, sems = refs[held:count], refs[count : 2 * count - held], refs[-1]
    targets = refs[2 * count - held : -1]
    copies = [pltpu.make_async_copy(f, n, sems.at[i]) for i, (f, n) in enumerate(zip(far, near, strict=True))]
    for copy in copies:
        copy.start()
    for i, (source, target) in enumerate(zip((*refs[:held], *near), targets)):
        if i >= held:
            copies[i - held].wait()
        rows, width = source.shape

        def body(i, _, source=source, target=target):
            at = pl.ds(pl.multiple_of(i * TURN, TURN), TURN)
            target[at, :] = source[:, at].T
            return 0

        lax.fori_loop(0, width // TURN, body, 0)
    for copy in copies[max(0, len(targets) - held) :]:
        copy.wait()


def turn(after, held, far, turned):
    vmem = pl.BlockSpec(memory_space=pltpu.VMEM)
    weights = (*held, *far)
    total = sum(w.size * w.dtype.itemsize for w in (*far, *weights[:turned], *weights[:turned]))
    out = pl.pallas_call(
        functools.partial(turn_kernel, len(held), len(weights)),
        out_shape=[pltpu.VMEM(w.shape, w.dtype) for w in far]
        + [pltpu.VMEM(w.shape[::-1], w.dtype) for w in weights[:turned]],
        in_specs=[vmem] * (1 + len(held)) + [pl.BlockSpec(memory_space=pltpu.HBM)] * len(far),
        out_specs=[vmem] * (len(far) + turned),
        scratch_shapes=[pltpu.SemaphoreType.DMA((max(1, len(far)),))],
        compiler_params=pltpu.CompilerParams(vmem_limit_bytes=LOAD_VMEM),
        cost_estimate=pl.CostEstimate(flops=0, bytes_accessed=total, transcendentals=0),
        name="turn",
    )(after, *held, *[pltpu.with_memory_space_constraint(w, pltpu.HBM) for w in far])
    return out[: len(far)], out[len(far) :]


def swiglu_kernel(*refs):
    count = (len(refs) - 5) // 2
    pieces, (gate_ref, up_ref, down_ref, *turned), results = refs[:count], refs[count : count + 5], refs[count + 5 :]
    width = gate_ref.shape[1]
    rows_x = jnp.concatenate([p[:, :width] for p in pieces], axis=0)
    rows_g = jnp.concatenate([p[:, width:] for p in pieces], axis=0)
    pre_gate = jnp.dot(rows_x, turned[0][...], preferred_element_type=jnp.float32)
    pre_up = jnp.dot(rows_x, turned[1][...], preferred_element_type=jnp.float32)
    d_hidden = lax.dot_general(rows_g, down_ref[...], CONTRACT_LAST, preferred_element_type=jnp.float32)
    logistic = jax.nn.sigmoid(pre_gate)
    activated = pre_gate * logistic
    hidden = (activated * pre_up).astype(jnp.bfloat16)
    grad_gate = (d_hidden * pre_up * logistic * (1.0 + pre_gate * (1.0 - logistic))).astype(jnp.bfloat16)
    grad_up = (d_hidden * activated).astype(jnp.bfloat16)
    step = 512
    for at in range(0, width, step):
        part = jnp.dot(hidden, down_ref[:, at : at + step], preferred_element_type=jnp.float32)
        grad = jnp.dot(grad_gate, gate_ref[:, at : at + step], preferred_element_type=jnp.float32)
        grad = grad + jnp.dot(grad_up, up_ref[:, at : at + step], preferred_element_type=jnp.float32)
        first = 0
        for result in results:
            rows = result.shape[0]
            result[:, at : at + step] = part[first : first + rows].astype(jnp.bfloat16)
            result[:, width + at : width + at + step] = grad[first : first + rows].astype(jnp.bfloat16)
            first += rows


def swiglu(pieces, weights, out_rows):
    both = pieces[0].shape[1]
    vmem = pl.BlockSpec(memory_space=pltpu.VMEM)
    rows = sum(out_rows)
    flops = 12 * rows * weights[0].size
    return pl.pallas_call(
        swiglu_kernel,
        out_shape=[jax.ShapeDtypeStruct((r, both), jnp.bfloat16) for r in out_rows],
        in_specs=[vmem] * (len(pieces) + len(weights)),
        out_specs=[vmem] * len(out_rows),
        compiler_params=pltpu.CompilerParams(vmem_limit_bytes=SWIGLU_VMEM),
        cost_estimate=pl.CostEstimate(flops=flops, bytes_accessed=6 * weights[0].size, transcendentals=0),
        name="swiglu",
    )(*pieces, *weights)


def dense_body(tokens, cotangent, routes, gate_wts, w_gate, w_up, w_down):
    blks = lax.axis_size("blk")
    members = lax.axis_size("member")
    blk = lax.axis_index("blk")
    member = lax.axis_index("member")
    _, rows, width = tokens.shape
    both = 2 * width
    column_rows = blks * rows
    apart = (6, 4, 2)

    def along_blk(value, by):
        return lax.ppermute(value, "blk", [(i, (i + by) % blks) for i in range(blks)])

    def across(value, bits):
        return lax.ppermute(value, "member", [(i, i ^ bits) for i in range(members)])

    first = load(w_gate[0], w_up[0])
    held = lax.optimization_barrier(jnp.concatenate([tokens[0], cotangent[0]], axis=1))
    column = jnp.concatenate([held] + [along_blk(held, k) for k in range(1, blks)], axis=0)
    rest, turned = turn(column, first, (w_down[0],), 2)
    weights = (*first, *rest)
    own = [column] + [across(column, bits) for bits in apart]
    own[1:] = lax.optimization_barrier((*own[1:], turned[0]))[:-1]
    other = [across(piece, 1) for piece in own]
    parts = swiglu(own + other, (*weights, *turned), [column_rows] * (2 * len(own)))
    own_part, other_part = parts[: len(own)], parts[len(own) :]
    summed = [
        (mine.astype(jnp.float32) + across(theirs, 1).astype(jnp.float32)).astype(jnp.bfloat16)
        for mine, theirs in zip(own_part, other_part, strict=True)
    ]
    back = [summed[0]] + [across(piece, bits) for piece, bits in zip(summed[1:], apart, strict=True)]

    places = ((blk - jnp.arange(blks)) % blks)[:, None] * rows + jnp.arange(rows)[None, :]
    slots = (member ^ jnp.array([0, *apart])) // 2
    experts = blk * EXP_GRP + slots
    at_place = places.reshape(-1)[None, :, None, None] == jnp.arange(column_rows)[None, None, :, None]
    named = routes[0][None, None] == experts[:, None, None, None]
    weight = jnp.sum(jnp.where(at_place & named, gate_wts[0][None, None], 0.0), axis=(2, 3))

    total = sum(piece.astype(jnp.float32) * weight[i][:, None] for i, piece in enumerate(back))
    total = total.reshape(blks, rows, both)
    sent = total.astype(jnp.bfloat16)
    result = total[0]
    for k in range(blks - 1, 0, -1):
        result = result + along_blk(sent[k], -k).astype(jnp.float32)
    result = result.astype(jnp.bfloat16)
    return result[None, :, :width], result[None, :, width:]


def slot_layout(route_ids, first_expert, capacity):
    local_ids = route_ids - first_expert
    slot_ids = jnp.arange(EXP_GRP, dtype=jnp.int32)
    matches = (local_ids[None, :, :] == slot_ids[:, None, None]).astype(jnp.int32)
    running = jnp.cumsum(matches.reshape(EXP_GRP, -1), axis=1).reshape(matches.shape) - 1
    places = jnp.arange(capacity, dtype=jnp.int32)
    chosen = (matches[:, None, :, :] == 1) & (running[:, None, :, :] == places[None, :, None, None])
    return chosen.astype(jnp.float32)


def expert_forward(row_block, gate_local, up_local, down_local):
    pre_gate = lax.dot_general(
        row_block, gate_local, CONTRACT_LAST, preferred_element_type=jnp.float32
    )
    pre_up = lax.dot_general(row_block, up_local, CONTRACT_LAST, preferred_element_type=jnp.float32)
    hidden = (pre_gate * jax.nn.sigmoid(pre_gate) * pre_up).astype(jnp.bfloat16)
    partial_value = jnp.dot(hidden, down_local, preferred_element_type=jnp.float32).astype(
        jnp.bfloat16
    )
    return (partial_value, pre_gate, pre_up)


def expert_backward(cot_rows, pre_gate, pre_up, gate_local, up_local, down_local):
    d_hidden = lax.dot_general(
        cot_rows, down_local, CONTRACT_LAST, preferred_element_type=jnp.float32
    )
    logistic = jax.nn.sigmoid(pre_gate)
    activated = pre_gate * logistic
    grad_gate = (d_hidden * pre_up * logistic * (1.0 + pre_gate * (1.0 - logistic))).astype(
        jnp.bfloat16
    )
    grad_up = (d_hidden * activated).astype(jnp.bfloat16)
    partial_value = jnp.dot(grad_gate, gate_local, preferred_element_type=jnp.float32)
    partial_value = partial_value + jnp.dot(grad_up, up_local, preferred_element_type=jnp.float32)
    return partial_value.astype(jnp.bfloat16)


def combine_rows(occupied, slot_weight, returned, shards):
    model_width = returned.shape[2]
    per_slot = jnp.sum(
        returned.astype(jnp.float32).reshape(EXP_GRP, shards, -1, model_width), axis=1
    )
    scaled = per_slot.reshape(-1, model_width) * slot_weight
    return lax.dot_general(
        occupied,
        scaled,
        CONTRACT_FIRST,
        precision=lax.Precision.HIGHEST,
        preferred_element_type=jnp.float32,
    )


def slot_body(tokens, cotangent, routes, gate_wts, w_gate, w_up, w_down):
    col_x, col_g = (
        lax.all_gather(tokens[0], "blk", axis=0, tiled=True),
        lax.all_gather(cotangent[0], "blk", axis=0, tiled=True),
    )
    model_width = col_x.shape[1]
    members = lax.axis_size("member")
    shards = members // EXP_GRP
    layout = slot_layout(routes[0], lax.axis_index("blk") * EXP_GRP, CAP)
    occupied = jnp.sum(layout, axis=3).reshape(EXP_GRP * CAP, -1)
    picker = occupied.astype(jnp.bfloat16)
    slot_weight = jnp.sum(layout * gate_wts[0][None, None, :, :], axis=(2, 3)).reshape(
        EXP_GRP * CAP, 1
    )
    send_x = jnp.dot(picker, col_x, preferred_element_type=jnp.float32).astype(jnp.bfloat16)
    send_g = jnp.dot(picker, col_g, preferred_element_type=jnp.float32).astype(jnp.bfloat16)
    send_x = jnp.repeat(send_x.reshape(EXP_GRP, CAP, model_width), shards, axis=0)
    send_g = jnp.repeat(send_g.reshape(EXP_GRP, CAP, model_width), shards, axis=0)
    gate_local = w_gate[0]
    up_local = w_up[0]
    down_local = w_down[0]
    arrived_x = lax.all_to_all(send_x, "member", split_axis=0, concat_axis=0, tiled=True)
    out_part, pre_gate, pre_up = expert_forward(
        arrived_x.reshape(-1, model_width), gate_local, up_local, down_local
    )
    back_out = lax.all_to_all(
        out_part.reshape(members, CAP, model_width),
        "member",
        split_axis=0,
        concat_axis=0,
        tiled=True,
    )
    arrived_g = lax.all_to_all(send_g, "member", split_axis=0, concat_axis=0, tiled=True)
    grad_part = expert_backward(
        arrived_g.reshape(-1, model_width), pre_gate, pre_up, gate_local, up_local, down_local
    )
    back_grad = lax.all_to_all(
        grad_part.reshape(members, CAP, model_width),
        "member",
        split_axis=0,
        concat_axis=0,
        tiled=True,
    )
    summed_out = combine_rows(occupied, slot_weight, back_out, shards)
    summed_grad = combine_rows(occupied, slot_weight, back_grad, shards)
    out_rows, grad_rows = (
        lax.psum_scatter(summed_out, "blk", scatter_dimension=0, tiled=True),
        lax.psum_scatter(summed_grad, "blk", scatter_dimension=0, tiled=True),
    )
    return (out_rows.astype(jnp.bfloat16)[None], grad_rows.astype(jnp.bfloat16)[None])


def solution(mesh):
    placed = (
        P("member", "blk", None),
        P("member", "blk", None),
        P("member", None, None),
        P("member", None, None),
        P("blk", "member", None),
        P("blk", "member", None),
        P("blk", "member", None),
    )

    def body(tokens, *rest):
        members = lax.axis_size("member")
        count = members * lax.axis_size("blk") * tokens.shape[1]
        dense = count <= DENSE_TOKENS and members == 2 * EXP_GRP
        return (dense_body if dense else slot_body)(tokens, *rest)

    return jax.shard_map(
        body,
        mesh=mesh,
        in_specs=placed,
        out_specs=(P("member", "blk", None), P("member", "blk", None)),
        check_vma=False,
    )
```

```python
import jax
import jax.numpy as jnp
from jax import lax
from jax.experimental import pallas as pl
from jax.experimental.pallas import tpu as pltpu
from jax.sharding import PartitionSpec as P

EXP_GRP = 4
CAP = 6
DENSE_TOKENS = 64
CHUNKS = 4
LOAD_VMEM = 1 << 20
TURN_VMEM = 8 << 20
SWIGLU_VMEM = 16 << 20

CONTRACT_LAST = (((1,), (1,)), ((), ()))
CONTRACT_FIRST = (((0,), (0,)), ((), ()))


def load_kernel(*refs):
    count = len(refs) // 2
    far, near, sems = refs[:count], refs[count:-1], refs[-1]
    parts = sems.shape[1]
    copies = []
    for i in range(count):
        span = far[i].shape[0] // parts
        for c in range(parts):
            at = pl.ds(c * span, span)
            copies.append(pltpu.make_async_copy(far[i].at[at], near[i].at[at], sems.at[i, c]))
    for copy in copies:
        copy.start()
    for copy in copies:
        copy.wait()


def load(*weights):
    total = sum(w.size * w.dtype.itemsize for w in weights)
    return pl.pallas_call(
        load_kernel,
        out_shape=[pltpu.VMEM(w.shape, w.dtype) for w in weights],
        in_specs=[pl.BlockSpec(memory_space=pltpu.HBM)] * len(weights),
        out_specs=[pl.BlockSpec(memory_space=pltpu.VMEM)] * len(weights),
        scratch_shapes=[pltpu.SemaphoreType.DMA((len(weights), CHUNKS))],
        compiler_params=pltpu.CompilerParams(vmem_limit_bytes=LOAD_VMEM),
        cost_estimate=pl.CostEstimate(flops=0, bytes_accessed=total, transcendentals=0),
        name="load",
    )(*[pltpu.with_memory_space_constraint(w, pltpu.HBM) for w in weights])


def turn_kernel(gate_ref, up_ref, far_ref, _, down_ref, gate_turned, up_turned, down_turned, sems):
    copy = pltpu.make_async_copy(far_ref, down_ref, sems.at[0])
    copy.start()
    gate_turned[...] = gate_ref[...].T
    up_turned[...] = up_ref[...].T
    copy.wait()
    down_turned[...] = down_ref[...].T


def turn(gate, up, down, after):
    vmem = pl.BlockSpec(memory_space=pltpu.VMEM)
    turned = [pltpu.VMEM(w.shape[::-1], w.dtype) for w in (gate, up, down)]
    total = 7 * down.size * down.dtype.itemsize
    return pl.pallas_call(
        turn_kernel,
        out_shape=[pltpu.VMEM(down.shape, down.dtype), *turned],
        in_specs=[vmem, vmem, pl.BlockSpec(memory_space=pltpu.HBM), vmem],
        out_specs=[vmem] * 4,
        scratch_shapes=[pltpu.SemaphoreType.DMA((1,))],
        compiler_params=pltpu.CompilerParams(vmem_limit_bytes=TURN_VMEM),
        cost_estimate=pl.CostEstimate(flops=0, bytes_accessed=total, transcendentals=0),
        name="turn",
    )(gate, up, pltpu.with_memory_space_constraint(down, pltpu.HBM), after)


def swiglu_kernel(*refs):
    count = (len(refs) - 6) // 2
    pieces, results = refs[:count], refs[count + 6 :]
    gate_ref, up_ref, down_ref, gate_turned, up_turned, down_turned = refs[count : count + 6]
    width = gate_ref.shape[1]
    rows_x = jnp.concatenate([p[:, :width] for p in pieces], axis=0)
    rows_g = jnp.concatenate([p[:, width:] for p in pieces], axis=0)
    pre_gate = jnp.dot(rows_x, gate_turned[...], preferred_element_type=jnp.float32)
    pre_up = jnp.dot(rows_x, up_turned[...], preferred_element_type=jnp.float32)
    d_hidden = jnp.dot(rows_g, down_turned[...], preferred_element_type=jnp.float32)
    logistic = jax.nn.sigmoid(pre_gate)
    activated = pre_gate * logistic
    hidden = (activated * pre_up).astype(jnp.bfloat16)
    grad_gate = (d_hidden * pre_up * logistic * (1.0 + pre_gate * (1.0 - logistic))).astype(jnp.bfloat16)
    grad_up = (d_hidden * activated).astype(jnp.bfloat16)
    step = 512
    for at in range(0, width, step):
        part = jnp.dot(hidden, down_ref[:, at : at + step], preferred_element_type=jnp.float32)
        grad = jnp.dot(grad_gate, gate_ref[:, at : at + step], preferred_element_type=jnp.float32)
        grad = grad + jnp.dot(grad_up, up_ref[:, at : at + step], preferred_element_type=jnp.float32)
        first = 0
        for result in results:
            rows = result.shape[0]
            result[:, at : at + step] = part[first : first + rows].astype(jnp.bfloat16)
            result[:, width + at : width + at + step] = grad[first : first + rows].astype(jnp.bfloat16)
            first += rows


def swiglu(pieces, weights, out_rows):
    both = pieces[0].shape[1]
    vmem = pl.BlockSpec(memory_space=pltpu.VMEM)
    rows = sum(out_rows)
    flops = 12 * rows * weights[0].size
    return pl.pallas_call(
        swiglu_kernel,
        out_shape=[jax.ShapeDtypeStruct((r, both), jnp.bfloat16) for r in out_rows],
        in_specs=[vmem] * (len(pieces) + len(weights)),
        out_specs=[vmem] * len(out_rows),
        compiler_params=pltpu.CompilerParams(vmem_limit_bytes=SWIGLU_VMEM),
        cost_estimate=pl.CostEstimate(flops=flops, bytes_accessed=6 * weights[0].size, transcendentals=0),
        name="swiglu",
    )(*pieces, *weights)


def dense_body(tokens, cotangent, routes, gate_wts, w_gate, w_up, w_down):
    blks = lax.axis_size("blk")
    members = lax.axis_size("member")
    blk = lax.axis_index("blk")
    member = lax.axis_index("member")
    _, rows, width = tokens.shape
    both = 2 * width
    column_rows = blks * rows
    apart = (6, 4, 2)

    def along_blk(value, by):
        return lax.ppermute(value, "blk", [(i, (i + by) % blks) for i in range(blks)])

    def across(value, bits):
        return lax.ppermute(value, "member", [(i, i ^ bits) for i in range(members)])

    gate, up = load(w_gate[0], w_up[0])
    held = lax.optimization_barrier(jnp.concatenate([tokens[0], cotangent[0]], axis=1))
    column = jnp.concatenate([held] + [along_blk(held, k) for k in range(1, blks)], axis=0)
    down, *turned = turn(gate, up, w_down[0], column)
    own = [column] + [across(column, bits) for bits in apart]
    own[1:] = lax.optimization_barrier((*own[1:], turned[0]))[:-1]
    other = [across(piece, 1) for piece in own]
    parts = swiglu(own + other, (gate, up, down, *turned), [column_rows] * (2 * len(own)))
    own_part, other_part = parts[: len(own)], parts[len(own) :]
    summed = [
        mine.astype(jnp.float32) + across(theirs, 1).astype(jnp.float32)
        for mine, theirs in zip(own_part, other_part, strict=True)
    ]
    back = [summed[0]]
    for piece, bits in zip(summed[1:], apart, strict=True):
        back.append(across(piece.astype(jnp.bfloat16), bits).astype(jnp.float32))

    places = ((blk - jnp.arange(blks)) % blks)[:, None] * rows + jnp.arange(rows)[None, :]
    slots = (member ^ jnp.array([0, *apart])) // 2
    experts = blk * EXP_GRP + slots
    at_place = places.reshape(-1)[None, :, None, None] == jnp.arange(column_rows)[None, None, :, None]
    named = routes[0][None, None] == experts[:, None, None, None]
    weight = jnp.sum(jnp.where(at_place & named, gate_wts[0][None, None], 0.0), axis=(2, 3))

    total = sum(piece * weight[i][:, None] for i, piece in enumerate(back))
    total = total.reshape(blks, rows, both)
    sent = total.astype(jnp.bfloat16)
    result = total[0]
    for k in range(blks - 1, 0, -1):
        result = result + along_blk(sent[k], -k).astype(jnp.float32)
    result = result.astype(jnp.bfloat16)
    return result[None, :, :width], result[None, :, width:]


def slot_layout(route_ids, first_expert, capacity):
    local_ids = route_ids - first_expert
    slot_ids = jnp.arange(EXP_GRP, dtype=jnp.int32)
    matches = (local_ids[None, :, :] == slot_ids[:, None, None]).astype(jnp.int32)
    running = jnp.cumsum(matches.reshape(EXP_GRP, -1), axis=1).reshape(matches.shape) - 1
    places = jnp.arange(capacity, dtype=jnp.int32)
    chosen = (matches[:, None, :, :] == 1) & (running[:, None, :, :] == places[None, :, None, None])
    return chosen.astype(jnp.float32)


def expert_forward(row_block, gate_local, up_local, down_local):
    pre_gate = lax.dot_general(
        row_block, gate_local, CONTRACT_LAST, preferred_element_type=jnp.float32
    )
    pre_up = lax.dot_general(row_block, up_local, CONTRACT_LAST, preferred_element_type=jnp.float32)
    hidden = (pre_gate * jax.nn.sigmoid(pre_gate) * pre_up).astype(jnp.bfloat16)
    partial_value = jnp.dot(hidden, down_local, preferred_element_type=jnp.float32).astype(
        jnp.bfloat16
    )
    return (partial_value, pre_gate, pre_up)


def expert_backward(cot_rows, pre_gate, pre_up, gate_local, up_local, down_local):
    d_hidden = lax.dot_general(
        cot_rows, down_local, CONTRACT_LAST, preferred_element_type=jnp.float32
    )
    logistic = jax.nn.sigmoid(pre_gate)
    activated = pre_gate * logistic
    grad_gate = (d_hidden * pre_up * logistic * (1.0 + pre_gate * (1.0 - logistic))).astype(
        jnp.bfloat16
    )
    grad_up = (d_hidden * activated).astype(jnp.bfloat16)
    partial_value = jnp.dot(grad_gate, gate_local, preferred_element_type=jnp.float32)
    partial_value = partial_value + jnp.dot(grad_up, up_local, preferred_element_type=jnp.float32)
    return partial_value.astype(jnp.bfloat16)


def combine_rows(occupied, slot_weight, returned, shards):
    model_width = returned.shape[2]
    per_slot = jnp.sum(
        returned.astype(jnp.float32).reshape(EXP_GRP, shards, -1, model_width), axis=1
    )
    scaled = per_slot.reshape(-1, model_width) * slot_weight
    return lax.dot_general(
        occupied,
        scaled,
        CONTRACT_FIRST,
        precision=lax.Precision.HIGHEST,
        preferred_element_type=jnp.float32,
    )


def slot_body(tokens, cotangent, routes, gate_wts, w_gate, w_up, w_down):
    col_x, col_g = (
        lax.all_gather(tokens[0], "blk", axis=0, tiled=True),
        lax.all_gather(cotangent[0], "blk", axis=0, tiled=True),
    )
    model_width = col_x.shape[1]
    members = lax.axis_size("member")
    shards = members // EXP_GRP
    layout = slot_layout(routes[0], lax.axis_index("blk") * EXP_GRP, CAP)
    occupied = jnp.sum(layout, axis=3).reshape(EXP_GRP * CAP, -1)
    picker = occupied.astype(jnp.bfloat16)
    slot_weight = jnp.sum(layout * gate_wts[0][None, None, :, :], axis=(2, 3)).reshape(
        EXP_GRP * CAP, 1
    )
    send_x = jnp.dot(picker, col_x, preferred_element_type=jnp.float32).astype(jnp.bfloat16)
    send_g = jnp.dot(picker, col_g, preferred_element_type=jnp.float32).astype(jnp.bfloat16)
    send_x = jnp.repeat(send_x.reshape(EXP_GRP, CAP, model_width), shards, axis=0)
    send_g = jnp.repeat(send_g.reshape(EXP_GRP, CAP, model_width), shards, axis=0)
    gate_local = w_gate[0]
    up_local = w_up[0]
    down_local = w_down[0]
    arrived_x = lax.all_to_all(send_x, "member", split_axis=0, concat_axis=0, tiled=True)
    out_part, pre_gate, pre_up = expert_forward(
        arrived_x.reshape(-1, model_width), gate_local, up_local, down_local
    )
    back_out = lax.all_to_all(
        out_part.reshape(members, CAP, model_width),
        "member",
        split_axis=0,
        concat_axis=0,
        tiled=True,
    )
    arrived_g = lax.all_to_all(send_g, "member", split_axis=0, concat_axis=0, tiled=True)
    grad_part = expert_backward(
        arrived_g.reshape(-1, model_width), pre_gate, pre_up, gate_local, up_local, down_local
    )
    back_grad = lax.all_to_all(
        grad_part.reshape(members, CAP, model_width),
        "member",
        split_axis=0,
        concat_axis=0,
        tiled=True,
    )
    summed_out = combine_rows(occupied, slot_weight, back_out, shards)
    summed_grad = combine_rows(occupied, slot_weight, back_grad, shards)
    out_rows, grad_rows = (
        lax.psum_scatter(summed_out, "blk", scatter_dimension=0, tiled=True),
        lax.psum_scatter(summed_grad, "blk", scatter_dimension=0, tiled=True),
    )
    return (out_rows.astype(jnp.bfloat16)[None], grad_rows.astype(jnp.bfloat16)[None])


def solution(mesh):
    placed = (
        P("member", "blk", None),
        P("member", "blk", None),
        P("member", None, None),
        P("member", None, None),
        P("blk", "member", None),
        P("blk", "member", None),
        P("blk", "member", None),
    )

    def body(tokens, *rest):
        members = lax.axis_size("member")
        count = members * lax.axis_size("blk") * tokens.shape[1]
        dense = count <= DENSE_TOKENS and members == 2 * EXP_GRP
        return (dense_body if dense else slot_body)(tokens, *rest)

    return jax.shard_map(
        body,
        mesh=mesh,
        in_specs=placed,
        out_specs=(P("member", "blk", None), P("member", "blk", None)),
        check_vma=False,
    )
```

```python
import jax
import jax.numpy as jnp
from jax import lax
from jax.experimental import pallas as pl
from jax.experimental.pallas import tpu as pltpu
from jax.sharding import PartitionSpec as P

EXP_GRP = 4
CAP = 6
DENSE_TOKENS = 64
CHUNKS = 4
LOAD_VMEM = 1 << 20
TURN_VMEM = 8 << 20
SWIGLU_VMEM = 16 << 20

CONTRACT_LAST = (((1,), (1,)), ((), ()))
CONTRACT_FIRST = (((0,), (0,)), ((), ()))


def load_kernel(*refs):
    count = len(refs) // 2
    far, near, sems = refs[:count], refs[count:-1], refs[-1]
    parts = sems.shape[1]
    copies = []
    for i in range(count):
        span = far[i].shape[0] // parts
        for c in range(parts):
            at = pl.ds(c * span, span)
            copies.append(pltpu.make_async_copy(far[i].at[at], near[i].at[at], sems.at[i, c]))
    for copy in copies:
        copy.start()
    for copy in copies:
        copy.wait()


def load(*weights):
    total = sum(w.size * w.dtype.itemsize for w in weights)
    return pl.pallas_call(
        load_kernel,
        out_shape=[pltpu.VMEM(w.shape, w.dtype) for w in weights],
        in_specs=[pl.BlockSpec(memory_space=pltpu.HBM)] * len(weights),
        out_specs=[pl.BlockSpec(memory_space=pltpu.VMEM)] * len(weights),
        scratch_shapes=[pltpu.SemaphoreType.DMA((len(weights), CHUNKS))],
        compiler_params=pltpu.CompilerParams(vmem_limit_bytes=LOAD_VMEM),
        cost_estimate=pl.CostEstimate(flops=0, bytes_accessed=total, transcendentals=0),
        name="load",
    )(*[pltpu.with_memory_space_constraint(w, pltpu.HBM) for w in weights])


def turn_kernel(gate_ref, up_ref, far_ref, _, down_ref, gate_turned, up_turned, down_turned, sems):
    copy = pltpu.make_async_copy(far_ref, down_ref, sems.at[0])
    copy.start()
    gate_turned[...] = gate_ref[...].T
    up_turned[...] = up_ref[...].T
    copy.wait()
    down_turned[...] = down_ref[...].T


def turn(gate, up, down, after):
    vmem = pl.BlockSpec(memory_space=pltpu.VMEM)
    turned = [pltpu.VMEM(w.shape[::-1], w.dtype) for w in (gate, up, down)]
    total = 7 * down.size * down.dtype.itemsize
    return pl.pallas_call(
        turn_kernel,
        out_shape=[pltpu.VMEM(down.shape, down.dtype), *turned],
        in_specs=[vmem, vmem, pl.BlockSpec(memory_space=pltpu.HBM), vmem],
        out_specs=[vmem] * 4,
        scratch_shapes=[pltpu.SemaphoreType.DMA((1,))],
        compiler_params=pltpu.CompilerParams(vmem_limit_bytes=TURN_VMEM),
        cost_estimate=pl.CostEstimate(flops=0, bytes_accessed=total, transcendentals=0),
        name="turn",
    )(gate, up, pltpu.with_memory_space_constraint(down, pltpu.HBM), after)


def swiglu_kernel(*refs):
    count = (len(refs) - 6) // 2
    pieces, results = refs[:count], refs[count + 6 :]
    gate_ref, up_ref, down_ref, gate_turned, up_turned, down_turned = refs[count : count + 6]
    width = gate_ref.shape[1]
    rows_x = jnp.concatenate([p[:, :width] for p in pieces], axis=0)
    rows_g = jnp.concatenate([p[:, width:] for p in pieces], axis=0)
    pre_gate = jnp.dot(rows_x, gate_turned[...], preferred_element_type=jnp.float32)
    pre_up = jnp.dot(rows_x, up_turned[...], preferred_element_type=jnp.float32)
    d_hidden = jnp.dot(rows_g, down_turned[...], preferred_element_type=jnp.float32)
    logistic = jax.nn.sigmoid(pre_gate)
    activated = pre_gate * logistic
    hidden = (activated * pre_up).astype(jnp.bfloat16)
    grad_gate = (d_hidden * pre_up * logistic * (1.0 + pre_gate * (1.0 - logistic))).astype(jnp.bfloat16)
    grad_up = (d_hidden * activated).astype(jnp.bfloat16)
    step = 512
    for at in range(0, width, step):
        part = jnp.dot(hidden, down_ref[:, at : at + step], preferred_element_type=jnp.float32)
        grad = jnp.dot(grad_gate, gate_ref[:, at : at + step], preferred_element_type=jnp.float32)
        grad = grad + jnp.dot(grad_up, up_ref[:, at : at + step], preferred_element_type=jnp.float32)
        first = 0
        for result in results:
            rows = result.shape[0]
            result[:, at : at + step] = part[first : first + rows].astype(jnp.bfloat16)
            result[:, width + at : width + at + step] = grad[first : first + rows].astype(jnp.bfloat16)
            first += rows


def swiglu(pieces, weights, out_rows):
    both = pieces[0].shape[1]
    vmem = pl.BlockSpec(memory_space=pltpu.VMEM)
    rows = sum(out_rows)
    flops = 12 * rows * weights[0].size
    return pl.pallas_call(
        swiglu_kernel,
        out_shape=[jax.ShapeDtypeStruct((r, both), jnp.bfloat16) for r in out_rows],
        in_specs=[vmem] * (len(pieces) + len(weights)),
        out_specs=[vmem] * len(out_rows),
        compiler_params=pltpu.CompilerParams(vmem_limit_bytes=SWIGLU_VMEM),
        cost_estimate=pl.CostEstimate(flops=flops, bytes_accessed=6 * weights[0].size, transcendentals=0),
        name="swiglu",
    )(*pieces, *weights)


def dense_body(tokens, cotangent, routes, gate_wts, w_gate, w_up, w_down):
    blks = lax.axis_size("blk")
    members = lax.axis_size("member")
    blk = lax.axis_index("blk")
    member = lax.axis_index("member")
    _, rows, width = tokens.shape
    both = 2 * width
    column_rows = blks * rows
    apart = (6, 4, 2)

    def along_blk(value, by):
        return lax.ppermute(value, "blk", [(i, (i + by) % blks) for i in range(blks)])

    def across(value, bits):
        return lax.ppermute(value, "member", [(i, i ^ bits) for i in range(members)])

    gate, up = load(w_gate[0], w_up[0])
    held = lax.optimization_barrier(jnp.concatenate([tokens[0], cotangent[0]], axis=1))
    column = jnp.concatenate([held] + [along_blk(held, k) for k in range(1, blks)], axis=0)
    down, *turned = turn(gate, up, w_down[0], column)
    own = [column] + [across(column, bits) for bits in apart]
    own[1], turned[0] = lax.optimization_barrier((own[1], turned[0]))
    other = [across(piece, 1) for piece in own]
    parts = swiglu(own + other, (gate, up, down, *turned), [column_rows] * (2 * len(own)))
    own_part, other_part = parts[: len(own)], parts[len(own) :]
    summed = [
        mine.astype(jnp.float32) + across(theirs, 1).astype(jnp.float32)
        for mine, theirs in zip(own_part, other_part, strict=True)
    ]
    back = [summed[0]]
    for piece, bits in zip(summed[1:], apart, strict=True):
        back.append(across(piece.astype(jnp.bfloat16), bits).astype(jnp.float32))

    places = ((blk - jnp.arange(blks)) % blks)[:, None] * rows + jnp.arange(rows)[None, :]
    slots = (member ^ jnp.array([0, *apart])) // 2
    experts = blk * EXP_GRP + slots
    at_place = places.reshape(-1)[None, :, None, None] == jnp.arange(column_rows)[None, None, :, None]
    named = routes[0][None, None] == experts[:, None, None, None]
    weight = jnp.sum(jnp.where(at_place & named, gate_wts[0][None, None], 0.0), axis=(2, 3))

    total = sum(piece * weight[i][:, None] for i, piece in enumerate(back))
    total = total.reshape(blks, rows, both)
    sent = total.astype(jnp.bfloat16)
    result = total[0]
    for k in range(blks - 1, 0, -1):
        result = result + along_blk(sent[k], -k).astype(jnp.float32)
    result = result.astype(jnp.bfloat16)
    return result[None, :, :width], result[None, :, width:]


def slot_layout(route_ids, first_expert, capacity):
    local_ids = route_ids - first_expert
    slot_ids = jnp.arange(EXP_GRP, dtype=jnp.int32)
    matches = (local_ids[None, :, :] == slot_ids[:, None, None]).astype(jnp.int32)
    running = jnp.cumsum(matches.reshape(EXP_GRP, -1), axis=1).reshape(matches.shape) - 1
    places = jnp.arange(capacity, dtype=jnp.int32)
    chosen = (matches[:, None, :, :] == 1) & (running[:, None, :, :] == places[None, :, None, None])
    return chosen.astype(jnp.float32)


def expert_forward(row_block, gate_local, up_local, down_local):
    pre_gate = lax.dot_general(
        row_block, gate_local, CONTRACT_LAST, preferred_element_type=jnp.float32
    )
    pre_up = lax.dot_general(row_block, up_local, CONTRACT_LAST, preferred_element_type=jnp.float32)
    hidden = (pre_gate * jax.nn.sigmoid(pre_gate) * pre_up).astype(jnp.bfloat16)
    partial_value = jnp.dot(hidden, down_local, preferred_element_type=jnp.float32).astype(
        jnp.bfloat16
    )
    return (partial_value, pre_gate, pre_up)


def expert_backward(cot_rows, pre_gate, pre_up, gate_local, up_local, down_local):
    d_hidden = lax.dot_general(
        cot_rows, down_local, CONTRACT_LAST, preferred_element_type=jnp.float32
    )
    logistic = jax.nn.sigmoid(pre_gate)
    activated = pre_gate * logistic
    grad_gate = (d_hidden * pre_up * logistic * (1.0 + pre_gate * (1.0 - logistic))).astype(
        jnp.bfloat16
    )
    grad_up = (d_hidden * activated).astype(jnp.bfloat16)
    partial_value = jnp.dot(grad_gate, gate_local, preferred_element_type=jnp.float32)
    partial_value = partial_value + jnp.dot(grad_up, up_local, preferred_element_type=jnp.float32)
    return partial_value.astype(jnp.bfloat16)


def combine_rows(occupied, slot_weight, returned, shards):
    model_width = returned.shape[2]
    per_slot = jnp.sum(
        returned.astype(jnp.float32).reshape(EXP_GRP, shards, -1, model_width), axis=1
    )
    scaled = per_slot.reshape(-1, model_width) * slot_weight
    return lax.dot_general(
        occupied,
        scaled,
        CONTRACT_FIRST,
        precision=lax.Precision.HIGHEST,
        preferred_element_type=jnp.float32,
    )


def slot_body(tokens, cotangent, routes, gate_wts, w_gate, w_up, w_down):
    col_x, col_g = (
        lax.all_gather(tokens[0], "blk", axis=0, tiled=True),
        lax.all_gather(cotangent[0], "blk", axis=0, tiled=True),
    )
    model_width = col_x.shape[1]
    members = lax.axis_size("member")
    shards = members // EXP_GRP
    layout = slot_layout(routes[0], lax.axis_index("blk") * EXP_GRP, CAP)
    occupied = jnp.sum(layout, axis=3).reshape(EXP_GRP * CAP, -1)
    picker = occupied.astype(jnp.bfloat16)
    slot_weight = jnp.sum(layout * gate_wts[0][None, None, :, :], axis=(2, 3)).reshape(
        EXP_GRP * CAP, 1
    )
    send_x = jnp.dot(picker, col_x, preferred_element_type=jnp.float32).astype(jnp.bfloat16)
    send_g = jnp.dot(picker, col_g, preferred_element_type=jnp.float32).astype(jnp.bfloat16)
    send_x = jnp.repeat(send_x.reshape(EXP_GRP, CAP, model_width), shards, axis=0)
    send_g = jnp.repeat(send_g.reshape(EXP_GRP, CAP, model_width), shards, axis=0)
    gate_local = w_gate[0]
    up_local = w_up[0]
    down_local = w_down[0]
    arrived_x = lax.all_to_all(send_x, "member", split_axis=0, concat_axis=0, tiled=True)
    out_part, pre_gate, pre_up = expert_forward(
        arrived_x.reshape(-1, model_width), gate_local, up_local, down_local
    )
    back_out = lax.all_to_all(
        out_part.reshape(members, CAP, model_width),
        "member",
        split_axis=0,
        concat_axis=0,
        tiled=True,
    )
    arrived_g = lax.all_to_all(send_g, "member", split_axis=0, concat_axis=0, tiled=True)
    grad_part = expert_backward(
        arrived_g.reshape(-1, model_width), pre_gate, pre_up, gate_local, up_local, down_local
    )
    back_grad = lax.all_to_all(
        grad_part.reshape(members, CAP, model_width),
        "member",
        split_axis=0,
        concat_axis=0,
        tiled=True,
    )
    summed_out = combine_rows(occupied, slot_weight, back_out, shards)
    summed_grad = combine_rows(occupied, slot_weight, back_grad, shards)
    out_rows, grad_rows = (
        lax.psum_scatter(summed_out, "blk", scatter_dimension=0, tiled=True),
        lax.psum_scatter(summed_grad, "blk", scatter_dimension=0, tiled=True),
    )
    return (out_rows.astype(jnp.bfloat16)[None], grad_rows.astype(jnp.bfloat16)[None])


def solution(mesh):
    placed = (
        P("member", "blk", None),
        P("member", "blk", None),
        P("member", None, None),
        P("member", None, None),
        P("blk", "member", None),
        P("blk", "member", None),
        P("blk", "member", None),
    )

    def body(tokens, *rest):
        members = lax.axis_size("member")
        count = members * lax.axis_size("blk") * tokens.shape[1]
        dense = count <= DENSE_TOKENS and members == 2 * EXP_GRP
        return (dense_body if dense else slot_body)(tokens, *rest)

    return jax.shard_map(
        body,
        mesh=mesh,
        in_specs=placed,
        out_specs=(P("member", "blk", None), P("member", "blk", None)),
        check_vma=False,
    )
```

```python
import jax
import jax.numpy as jnp
from jax import lax
from jax.experimental import pallas as pl
from jax.experimental.pallas import tpu as pltpu
from jax.sharding import PartitionSpec as P

EXP_GRP = 4
CAP = 6
DENSE_TOKENS = 64
CHUNKS = 4
LOAD_VMEM = 1 << 20
TURN_VMEM = 8 << 20
SWIGLU_VMEM = 16 << 20

CONTRACT_LAST = (((1,), (1,)), ((), ()))
CONTRACT_FIRST = (((0,), (0,)), ((), ()))


def load_kernel(*refs):
    count = len(refs) // 2
    far, near, sems = refs[:count], refs[count:-1], refs[-1]
    parts = sems.shape[1]
    copies = []
    for i in range(count):
        span = far[i].shape[0] // parts
        for c in range(parts):
            at = pl.ds(c * span, span)
            copies.append(pltpu.make_async_copy(far[i].at[at], near[i].at[at], sems.at[i, c]))
    for copy in copies:
        copy.start()
    for copy in copies:
        copy.wait()


def load(*weights):
    total = sum(w.size * w.dtype.itemsize for w in weights)
    return pl.pallas_call(
        load_kernel,
        out_shape=[pltpu.VMEM(w.shape, w.dtype) for w in weights],
        in_specs=[pl.BlockSpec(memory_space=pltpu.HBM)] * len(weights),
        out_specs=[pl.BlockSpec(memory_space=pltpu.VMEM)] * len(weights),
        scratch_shapes=[pltpu.SemaphoreType.DMA((len(weights), CHUNKS))],
        compiler_params=pltpu.CompilerParams(vmem_limit_bytes=LOAD_VMEM),
        cost_estimate=pl.CostEstimate(flops=0, bytes_accessed=total, transcendentals=0),
        name="load",
    )(*[pltpu.with_memory_space_constraint(w, pltpu.HBM) for w in weights])


def turn_kernel(gate_ref, up_ref, far_ref, _, down_ref, gate_turned, up_turned, down_turned, sems):
    copy = pltpu.make_async_copy(far_ref, down_ref, sems.at[0])
    copy.start()
    gate_turned[...] = gate_ref[...].T
    up_turned[...] = up_ref[...].T
    copy.wait()
    down_turned[...] = down_ref[...].T


def turn(gate, up, down, after):
    vmem = pl.BlockSpec(memory_space=pltpu.VMEM)
    turned = [pltpu.VMEM(w.shape[::-1], w.dtype) for w in (gate, up, down)]
    total = 7 * down.size * down.dtype.itemsize
    return pl.pallas_call(
        turn_kernel,
        out_shape=[pltpu.VMEM(down.shape, down.dtype), *turned],
        in_specs=[vmem, vmem, pl.BlockSpec(memory_space=pltpu.HBM), vmem],
        out_specs=[vmem] * 4,
        scratch_shapes=[pltpu.SemaphoreType.DMA((1,))],
        compiler_params=pltpu.CompilerParams(vmem_limit_bytes=TURN_VMEM),
        cost_estimate=pl.CostEstimate(flops=0, bytes_accessed=total, transcendentals=0),
        name="turn",
    )(gate, up, pltpu.with_memory_space_constraint(down, pltpu.HBM), after)


def swiglu_kernel(*refs):
    count = (len(refs) - 6) // 2
    pieces, results = refs[:count], refs[count + 6 :]
    gate_ref, up_ref, down_ref, gate_turned, up_turned, down_turned = refs[count : count + 6]
    width = gate_ref.shape[1]
    rows_x = jnp.concatenate([p[:, :width] for p in pieces], axis=0)
    rows_g = jnp.concatenate([p[:, width:] for p in pieces], axis=0)
    pre_gate = jnp.dot(rows_x, gate_turned[...], preferred_element_type=jnp.float32)
    pre_up = jnp.dot(rows_x, up_turned[...], preferred_element_type=jnp.float32)
    d_hidden = jnp.dot(rows_g, down_turned[...], preferred_element_type=jnp.float32)
    logistic = jax.nn.sigmoid(pre_gate)
    activated = pre_gate * logistic
    hidden = (activated * pre_up).astype(jnp.bfloat16)
    grad_gate = (d_hidden * pre_up * logistic * (1.0 + pre_gate * (1.0 - logistic))).astype(jnp.bfloat16)
    grad_up = (d_hidden * activated).astype(jnp.bfloat16)
    step = 512
    for at in range(0, width, step):
        part = jnp.dot(hidden, down_ref[:, at : at + step], preferred_element_type=jnp.float32)
        grad = jnp.dot(grad_gate, gate_ref[:, at : at + step], preferred_element_type=jnp.float32)
        grad = grad + jnp.dot(grad_up, up_ref[:, at : at + step], preferred_element_type=jnp.float32)
        first = 0
        for result in results:
            rows = result.shape[0]
            result[:, at : at + step] = part[first : first + rows].astype(jnp.bfloat16)
            result[:, width + at : width + at + step] = grad[first : first + rows].astype(jnp.bfloat16)
            first += rows


def swiglu(pieces, weights, out_rows):
    both = pieces[0].shape[1]
    vmem = pl.BlockSpec(memory_space=pltpu.VMEM)
    rows = sum(out_rows)
    flops = 12 * rows * weights[0].size
    return pl.pallas_call(
        swiglu_kernel,
        out_shape=[jax.ShapeDtypeStruct((r, both), jnp.bfloat16) for r in out_rows],
        in_specs=[vmem] * (len(pieces) + len(weights)),
        out_specs=[vmem] * len(out_rows),
        compiler_params=pltpu.CompilerParams(vmem_limit_bytes=SWIGLU_VMEM),
        cost_estimate=pl.CostEstimate(flops=flops, bytes_accessed=6 * weights[0].size, transcendentals=0),
        name="swiglu",
    )(*pieces, *weights)


def dense_body(tokens, cotangent, routes, gate_wts, w_gate, w_up, w_down):
    blks = lax.axis_size("blk")
    members = lax.axis_size("member")
    blk = lax.axis_index("blk")
    member = lax.axis_index("member")
    _, rows, width = tokens.shape
    both = 2 * width
    column_rows = blks * rows
    apart = (6, 4, 2)

    def along_blk(value, by):
        return lax.ppermute(value, "blk", [(i, (i + by) % blks) for i in range(blks)])

    def across(value, bits):
        return lax.ppermute(value, "member", [(i, i ^ bits) for i in range(members)])

    gate, up = load(w_gate[0], w_up[0])
    held = lax.optimization_barrier(jnp.concatenate([tokens[0], cotangent[0]], axis=1))
    column = jnp.concatenate([held] + [along_blk(held, k) for k in range(1, blks)], axis=0)
    down, *turned = turn(gate, up, w_down[0], column)
    own = [column] + [across(column, bits) for bits in apart]
    own[1], turned[0] = lax.optimization_barrier((own[1], turned[0]))
    other = [across(piece, 1) for piece in own]
    parts = swiglu(own + other, (gate, up, down, *turned), [column_rows] * (2 * len(own)))
    own_part, other_part = parts[: len(own)], parts[len(own) :]
    back = []
    for mine, theirs, bits in zip(own_part[1:], other_part[1:], apart, strict=True):
        piece = mine.astype(jnp.float32) + across(theirs, 1).astype(jnp.float32)
        back.append(across(piece.astype(jnp.bfloat16), bits))
    back[0], theirs = lax.optimization_barrier((back[0], other_part[0]))
    back = [piece.astype(jnp.float32) for piece in back]
    back.insert(0, own_part[0].astype(jnp.float32) + across(theirs, 1).astype(jnp.float32))

    places = ((blk - jnp.arange(blks)) % blks)[:, None] * rows + jnp.arange(rows)[None, :]
    slots = (member ^ jnp.array([0, *apart])) // 2
    experts = blk * EXP_GRP + slots
    at_place = places.reshape(-1)[None, :, None, None] == jnp.arange(column_rows)[None, None, :, None]
    named = routes[0][None, None] == experts[:, None, None, None]
    weight = jnp.sum(jnp.where(at_place & named, gate_wts[0][None, None], 0.0), axis=(2, 3))

    total = sum(piece * weight[i][:, None] for i, piece in enumerate(back))
    total = total.reshape(blks, rows, both)
    sent = total.astype(jnp.bfloat16)
    result = total[0]
    for k in range(blks - 1, 0, -1):
        result = result + along_blk(sent[k], -k).astype(jnp.float32)
    result = result.astype(jnp.bfloat16)
    return result[None, :, :width], result[None, :, width:]


def slot_layout(route_ids, first_expert, capacity):
    local_ids = route_ids - first_expert
    slot_ids = jnp.arange(EXP_GRP, dtype=jnp.int32)
    matches = (local_ids[None, :, :] == slot_ids[:, None, None]).astype(jnp.int32)
    running = jnp.cumsum(matches.reshape(EXP_GRP, -1), axis=1).reshape(matches.shape) - 1
    places = jnp.arange(capacity, dtype=jnp.int32)
    chosen = (matches[:, None, :, :] == 1) & (running[:, None, :, :] == places[None, :, None, None])
    return chosen.astype(jnp.float32)


def expert_forward(row_block, gate_local, up_local, down_local):
    pre_gate = lax.dot_general(
        row_block, gate_local, CONTRACT_LAST, preferred_element_type=jnp.float32
    )
    pre_up = lax.dot_general(row_block, up_local, CONTRACT_LAST, preferred_element_type=jnp.float32)
    hidden = (pre_gate * jax.nn.sigmoid(pre_gate) * pre_up).astype(jnp.bfloat16)
    partial_value = jnp.dot(hidden, down_local, preferred_element_type=jnp.float32).astype(
        jnp.bfloat16
    )
    return (partial_value, pre_gate, pre_up)


def expert_backward(cot_rows, pre_gate, pre_up, gate_local, up_local, down_local):
    d_hidden = lax.dot_general(
        cot_rows, down_local, CONTRACT_LAST, preferred_element_type=jnp.float32
    )
    logistic = jax.nn.sigmoid(pre_gate)
    activated = pre_gate * logistic
    grad_gate = (d_hidden * pre_up * logistic * (1.0 + pre_gate * (1.0 - logistic))).astype(
        jnp.bfloat16
    )
    grad_up = (d_hidden * activated).astype(jnp.bfloat16)
    partial_value = jnp.dot(grad_gate, gate_local, preferred_element_type=jnp.float32)
    partial_value = partial_value + jnp.dot(grad_up, up_local, preferred_element_type=jnp.float32)
    return partial_value.astype(jnp.bfloat16)


def combine_rows(occupied, slot_weight, returned, shards):
    model_width = returned.shape[2]
    per_slot = jnp.sum(
        returned.astype(jnp.float32).reshape(EXP_GRP, shards, -1, model_width), axis=1
    )
    scaled = per_slot.reshape(-1, model_width) * slot_weight
    return lax.dot_general(
        occupied,
        scaled,
        CONTRACT_FIRST,
        precision=lax.Precision.HIGHEST,
        preferred_element_type=jnp.float32,
    )


def slot_body(tokens, cotangent, routes, gate_wts, w_gate, w_up, w_down):
    col_x, col_g = (
        lax.all_gather(tokens[0], "blk", axis=0, tiled=True),
        lax.all_gather(cotangent[0], "blk", axis=0, tiled=True),
    )
    model_width = col_x.shape[1]
    members = lax.axis_size("member")
    shards = members // EXP_GRP
    layout = slot_layout(routes[0], lax.axis_index("blk") * EXP_GRP, CAP)
    occupied = jnp.sum(layout, axis=3).reshape(EXP_GRP * CAP, -1)
    picker = occupied.astype(jnp.bfloat16)
    slot_weight = jnp.sum(layout * gate_wts[0][None, None, :, :], axis=(2, 3)).reshape(
        EXP_GRP * CAP, 1
    )
    send_x = jnp.dot(picker, col_x, preferred_element_type=jnp.float32).astype(jnp.bfloat16)
    send_g = jnp.dot(picker, col_g, preferred_element_type=jnp.float32).astype(jnp.bfloat16)
    send_x = jnp.repeat(send_x.reshape(EXP_GRP, CAP, model_width), shards, axis=0)
    send_g = jnp.repeat(send_g.reshape(EXP_GRP, CAP, model_width), shards, axis=0)
    gate_local = w_gate[0]
    up_local = w_up[0]
    down_local = w_down[0]
    arrived_x = lax.all_to_all(send_x, "member", split_axis=0, concat_axis=0, tiled=True)
    out_part, pre_gate, pre_up = expert_forward(
        arrived_x.reshape(-1, model_width), gate_local, up_local, down_local
    )
    back_out = lax.all_to_all(
        out_part.reshape(members, CAP, model_width),
        "member",
        split_axis=0,
        concat_axis=0,
        tiled=True,
    )
    arrived_g = lax.all_to_all(send_g, "member", split_axis=0, concat_axis=0, tiled=True)
    grad_part = expert_backward(
        arrived_g.reshape(-1, model_width), pre_gate, pre_up, gate_local, up_local, down_local
    )
    back_grad = lax.all_to_all(
        grad_part.reshape(members, CAP, model_width),
        "member",
        split_axis=0,
        concat_axis=0,
        tiled=True,
    )
    summed_out = combine_rows(occupied, slot_weight, back_out, shards)
    summed_grad = combine_rows(occupied, slot_weight, back_grad, shards)
    out_rows, grad_rows = (
        lax.psum_scatter(summed_out, "blk", scatter_dimension=0, tiled=True),
        lax.psum_scatter(summed_grad, "blk", scatter_dimension=0, tiled=True),
    )
    return (out_rows.astype(jnp.bfloat16)[None], grad_rows.astype(jnp.bfloat16)[None])


def solution(mesh):
    placed = (
        P("member", "blk", None),
        P("member", "blk", None),
        P("member", None, None),
        P("member", None, None),
        P("blk", "member", None),
        P("blk", "member", None),
        P("blk", "member", None),
    )

    def body(tokens, *rest):
        members = lax.axis_size("member")
        count = members * lax.axis_size("blk") * tokens.shape[1]
        dense = count <= DENSE_TOKENS and members == 2 * EXP_GRP
        return (dense_body if dense else slot_body)(tokens, *rest)

    return jax.shard_map(
        body,
        mesh=mesh,
        in_specs=placed,
        out_specs=(P("member", "blk", None), P("member", "blk", None)),
        check_vma=False,
    )
```

```python
import jax
import jax.numpy as jnp
from jax import lax
from jax.experimental import pallas as pl
from jax.experimental.pallas import tpu as pltpu
from jax.sharding import PartitionSpec as P

EXP_GRP = 4
CAP = 6
DENSE_TOKENS = 64
CHUNKS = 4
LOAD_VMEM = 1 << 20
TURN_VMEM = 8 << 20
SWIGLU_VMEM = 16 << 20

CONTRACT_LAST = (((1,), (1,)), ((), ()))
CONTRACT_FIRST = (((0,), (0,)), ((), ()))


def load_kernel(*refs):
    count = len(refs) // 2
    far, near, sems = refs[:count], refs[count:-1], refs[-1]
    parts = sems.shape[1]
    copies = []
    for i in range(count):
        span = far[i].shape[0] // parts
        for c in range(parts):
            at = pl.ds(c * span, span)
            copies.append(pltpu.make_async_copy(far[i].at[at], near[i].at[at], sems.at[i, c]))
    for copy in copies:
        copy.start()
    for copy in copies:
        copy.wait()


def load(*weights):
    total = sum(w.size * w.dtype.itemsize for w in weights)
    return pl.pallas_call(
        load_kernel,
        out_shape=[pltpu.VMEM(w.shape, w.dtype) for w in weights],
        in_specs=[pl.BlockSpec(memory_space=pltpu.HBM)] * len(weights),
        out_specs=[pl.BlockSpec(memory_space=pltpu.VMEM)] * len(weights),
        scratch_shapes=[pltpu.SemaphoreType.DMA((len(weights), CHUNKS))],
        compiler_params=pltpu.CompilerParams(vmem_limit_bytes=LOAD_VMEM),
        cost_estimate=pl.CostEstimate(flops=0, bytes_accessed=total, transcendentals=0),
        name="load",
    )(*[pltpu.with_memory_space_constraint(w, pltpu.HBM) for w in weights])


def turn_kernel(gate_ref, up_ref, far_ref, _, down_ref, gate_turned, up_turned, down_turned, sems):
    copy = pltpu.make_async_copy(far_ref, down_ref, sems.at[0])
    copy.start()
    gate_turned[...] = gate_ref[...].T
    up_turned[...] = up_ref[...].T
    copy.wait()
    down_turned[...] = down_ref[...].T


def turn(gate, up, down, after):
    vmem = pl.BlockSpec(memory_space=pltpu.VMEM)
    turned = [pltpu.VMEM(w.shape[::-1], w.dtype) for w in (gate, up, down)]
    total = 7 * down.size * down.dtype.itemsize
    return pl.pallas_call(
        turn_kernel,
        out_shape=[pltpu.VMEM(down.shape, down.dtype), *turned],
        in_specs=[vmem, vmem, pl.BlockSpec(memory_space=pltpu.HBM), vmem],
        out_specs=[vmem] * 4,
        scratch_shapes=[pltpu.SemaphoreType.DMA((1,))],
        compiler_params=pltpu.CompilerParams(vmem_limit_bytes=TURN_VMEM),
        cost_estimate=pl.CostEstimate(flops=0, bytes_accessed=total, transcendentals=0),
        name="turn",
    )(gate, up, pltpu.with_memory_space_constraint(down, pltpu.HBM), after)


def swiglu_kernel(*refs):
    count = (len(refs) - 6) // 2
    pieces, results = refs[:count], refs[count + 6 :]
    gate_ref, up_ref, down_ref, gate_turned, up_turned, down_turned = refs[count : count + 6]
    width = gate_ref.shape[1]
    rows_x = jnp.concatenate([p[:, :width] for p in pieces], axis=0)
    rows_g = jnp.concatenate([p[:, width:] for p in pieces], axis=0)
    pre_gate = jnp.dot(rows_x, gate_turned[...], preferred_element_type=jnp.float32)
    pre_up = jnp.dot(rows_x, up_turned[...], preferred_element_type=jnp.float32)
    d_hidden = jnp.dot(rows_g, down_turned[...], preferred_element_type=jnp.float32)
    logistic = jax.nn.sigmoid(pre_gate)
    activated = pre_gate * logistic
    hidden = (activated * pre_up).astype(jnp.bfloat16)
    grad_gate = (d_hidden * pre_up * logistic * (1.0 + pre_gate * (1.0 - logistic))).astype(jnp.bfloat16)
    grad_up = (d_hidden * activated).astype(jnp.bfloat16)
    step = 512
    for at in range(0, width, step):
        part = jnp.dot(hidden, down_ref[:, at : at + step], preferred_element_type=jnp.float32)
        grad = jnp.dot(grad_gate, gate_ref[:, at : at + step], preferred_element_type=jnp.float32)
        grad = grad + jnp.dot(grad_up, up_ref[:, at : at + step], preferred_element_type=jnp.float32)
        first = 0
        for result in results:
            rows = result.shape[0]
            result[:, at : at + step] = part[first : first + rows].astype(jnp.bfloat16)
            result[:, width + at : width + at + step] = grad[first : first + rows].astype(jnp.bfloat16)
            first += rows


def swiglu(pieces, weights, out_rows):
    both = pieces[0].shape[1]
    vmem = pl.BlockSpec(memory_space=pltpu.VMEM)
    rows = sum(out_rows)
    flops = 12 * rows * weights[0].size
    return pl.pallas_call(
        swiglu_kernel,
        out_shape=[jax.ShapeDtypeStruct((r, both), jnp.bfloat16) for r in out_rows],
        in_specs=[vmem] * (len(pieces) + len(weights)),
        out_specs=[vmem] * len(out_rows),
        compiler_params=pltpu.CompilerParams(vmem_limit_bytes=SWIGLU_VMEM),
        cost_estimate=pl.CostEstimate(flops=flops, bytes_accessed=6 * weights[0].size, transcendentals=0),
        name="swiglu",
    )(*pieces, *weights)


def dense_body(tokens, cotangent, routes, gate_wts, w_gate, w_up, w_down):
    blks = lax.axis_size("blk")
    members = lax.axis_size("member")
    blk = lax.axis_index("blk")
    member = lax.axis_index("member")
    _, rows, width = tokens.shape
    both = 2 * width
    column_rows = blks * rows
    apart = (6, 2, 4)

    def along_blk(value, by):
        return lax.ppermute(value, "blk", [(i, (i + by) % blks) for i in range(blks)])

    def across(value, bits):
        return lax.ppermute(value, "member", [(i, i ^ bits) for i in range(members)])

    gate, up = load(w_gate[0], w_up[0])
    held = lax.optimization_barrier(jnp.concatenate([tokens[0], cotangent[0]], axis=1))
    column = jnp.concatenate([held] + [along_blk(held, k) for k in range(1, blks)], axis=0)
    down, *turned = turn(gate, up, w_down[0], column)
    own = [column] + [across(column, bits) for bits in apart]
    own[1], turned[0] = lax.optimization_barrier((own[1], turned[0]))
    other = [across(piece, 1) for piece in own]
    parts = swiglu(own + other, (gate, up, down, *turned), [column_rows] * (2 * len(own)))
    own_part, other_part = parts[: len(own)], parts[len(own) :]
    back = []
    for mine, theirs, bits in zip(own_part[1:], other_part[1:], apart, strict=True):
        piece = mine.astype(jnp.float32) + across(theirs, 1).astype(jnp.float32)
        back.append(across(piece.astype(jnp.bfloat16), bits))
    back[0], theirs = lax.optimization_barrier((back[0], other_part[0]))
    back = [piece.astype(jnp.float32) for piece in back]
    back.insert(0, own_part[0].astype(jnp.float32) + across(theirs, 1).astype(jnp.float32))

    places = ((blk - jnp.arange(blks)) % blks)[:, None] * rows + jnp.arange(rows)[None, :]
    slots = (member ^ jnp.array([0, *apart])) // 2
    experts = blk * EXP_GRP + slots
    at_place = places.reshape(-1)[None, :, None, None] == jnp.arange(column_rows)[None, None, :, None]
    named = routes[0][None, None] == experts[:, None, None, None]
    weight = jnp.sum(jnp.where(at_place & named, gate_wts[0][None, None], 0.0), axis=(2, 3))

    total = sum(piece * weight[i][:, None] for i, piece in enumerate(back))
    total = total.reshape(blks, rows, both)
    sent = total.astype(jnp.bfloat16)
    result = total[0]
    for k in range(blks - 1, 0, -1):
        result = result + along_blk(sent[k], -k).astype(jnp.float32)
    result = result.astype(jnp.bfloat16)
    return result[None, :, :width], result[None, :, width:]


def slot_layout(route_ids, first_expert, capacity):
    local_ids = route_ids - first_expert
    slot_ids = jnp.arange(EXP_GRP, dtype=jnp.int32)
    matches = (local_ids[None, :, :] == slot_ids[:, None, None]).astype(jnp.int32)
    running = jnp.cumsum(matches.reshape(EXP_GRP, -1), axis=1).reshape(matches.shape) - 1
    places = jnp.arange(capacity, dtype=jnp.int32)
    chosen = (matches[:, None, :, :] == 1) & (running[:, None, :, :] == places[None, :, None, None])
    return chosen.astype(jnp.float32)


def expert_forward(row_block, gate_local, up_local, down_local):
    pre_gate = lax.dot_general(
        row_block, gate_local, CONTRACT_LAST, preferred_element_type=jnp.float32
    )
    pre_up = lax.dot_general(row_block, up_local, CONTRACT_LAST, preferred_element_type=jnp.float32)
    hidden = (pre_gate * jax.nn.sigmoid(pre_gate) * pre_up).astype(jnp.bfloat16)
    partial_value = jnp.dot(hidden, down_local, preferred_element_type=jnp.float32).astype(
        jnp.bfloat16
    )
    return (partial_value, pre_gate, pre_up)


def expert_backward(cot_rows, pre_gate, pre_up, gate_local, up_local, down_local):
    d_hidden = lax.dot_general(
        cot_rows, down_local, CONTRACT_LAST, preferred_element_type=jnp.float32
    )
    logistic = jax.nn.sigmoid(pre_gate)
    activated = pre_gate * logistic
    grad_gate = (d_hidden * pre_up * logistic * (1.0 + pre_gate * (1.0 - logistic))).astype(
        jnp.bfloat16
    )
    grad_up = (d_hidden * activated).astype(jnp.bfloat16)
    partial_value = jnp.dot(grad_gate, gate_local, preferred_element_type=jnp.float32)
    partial_value = partial_value + jnp.dot(grad_up, up_local, preferred_element_type=jnp.float32)
    return partial_value.astype(jnp.bfloat16)


def combine_rows(occupied, slot_weight, returned, shards):
    model_width = returned.shape[2]
    per_slot = jnp.sum(
        returned.astype(jnp.float32).reshape(EXP_GRP, shards, -1, model_width), axis=1
    )
    scaled = per_slot.reshape(-1, model_width) * slot_weight
    return lax.dot_general(
        occupied,
        scaled,
        CONTRACT_FIRST,
        precision=lax.Precision.HIGHEST,
        preferred_element_type=jnp.float32,
    )


def slot_body(tokens, cotangent, routes, gate_wts, w_gate, w_up, w_down):
    col_x, col_g = (
        lax.all_gather(tokens[0], "blk", axis=0, tiled=True),
        lax.all_gather(cotangent[0], "blk", axis=0, tiled=True),
    )
    model_width = col_x.shape[1]
    members = lax.axis_size("member")
    shards = members // EXP_GRP
    layout = slot_layout(routes[0], lax.axis_index("blk") * EXP_GRP, CAP)
    occupied = jnp.sum(layout, axis=3).reshape(EXP_GRP * CAP, -1)
    picker = occupied.astype(jnp.bfloat16)
    slot_weight = jnp.sum(layout * gate_wts[0][None, None, :, :], axis=(2, 3)).reshape(
        EXP_GRP * CAP, 1
    )
    send_x = jnp.dot(picker, col_x, preferred_element_type=jnp.float32).astype(jnp.bfloat16)
    send_g = jnp.dot(picker, col_g, preferred_element_type=jnp.float32).astype(jnp.bfloat16)
    send_x = jnp.repeat(send_x.reshape(EXP_GRP, CAP, model_width), shards, axis=0)
    send_g = jnp.repeat(send_g.reshape(EXP_GRP, CAP, model_width), shards, axis=0)
    gate_local = w_gate[0]
    up_local = w_up[0]
    down_local = w_down[0]
    arrived_x = lax.all_to_all(send_x, "member", split_axis=0, concat_axis=0, tiled=True)
    out_part, pre_gate, pre_up = expert_forward(
        arrived_x.reshape(-1, model_width), gate_local, up_local, down_local
    )
    back_out = lax.all_to_all(
        out_part.reshape(members, CAP, model_width),
        "member",
        split_axis=0,
        concat_axis=0,
        tiled=True,
    )
    arrived_g = lax.all_to_all(send_g, "member", split_axis=0, concat_axis=0, tiled=True)
    grad_part = expert_backward(
        arrived_g.reshape(-1, model_width), pre_gate, pre_up, gate_local, up_local, down_local
    )
    back_grad = lax.all_to_all(
        grad_part.reshape(members, CAP, model_width),
        "member",
        split_axis=0,
        concat_axis=0,
        tiled=True,
    )
    summed_out = combine_rows(occupied, slot_weight, back_out, shards)
    summed_grad = combine_rows(occupied, slot_weight, back_grad, shards)
    out_rows, grad_rows = (
        lax.psum_scatter(summed_out, "blk", scatter_dimension=0, tiled=True),
        lax.psum_scatter(summed_grad, "blk", scatter_dimension=0, tiled=True),
    )
    return (out_rows.astype(jnp.bfloat16)[None], grad_rows.astype(jnp.bfloat16)[None])


def solution(mesh):
    placed = (
        P("member", "blk", None),
        P("member", "blk", None),
        P("member", None, None),
        P("member", None, None),
        P("blk", "member", None),
        P("blk", "member", None),
        P("blk", "member", None),
    )

    def body(tokens, *rest):
        members = lax.axis_size("member")
        count = members * lax.axis_size("blk") * tokens.shape[1]
        dense = count <= DENSE_TOKENS and members == 2 * EXP_GRP
        return (dense_body if dense else slot_body)(tokens, *rest)

    return jax.shard_map(
        body,
        mesh=mesh,
        in_specs=placed,
        out_specs=(P("member", "blk", None), P("member", "blk", None)),
        check_vma=False,
    )
```
